256 devices in a mesh: tm: 16 (over y_lo, x, core), space: 16 (over z, y_hi).
Axes of the slice: x: 4, y: 4 (y_hi: 2, y_lo: 2; y = y_hi * 2 + y_lo), z: 8, core: 2. Of those that a mesh axis runs over, the one named last changes fastest.
Arguments:
- states: bfloat16 [32, 64, 128, 256], P('tm', None, 'space'), may hold values from -6 to 6
- observed: bfloat16 [32, 64, 128, 256], P('tm', None, 'space'), may hold values from -6 to 6
- station_mask: int32 [32, 128, 256], P('tm', 'space'), may hold values 0 or 1
- noise: float32 [32, 64, 128, 256], P('tm', None, 'space'), may hold values from -6 to 6
- sigma_now: float32 [1], replicated, may hold values from 0.8 to 1.2
- sigma_next: float32 [1], replicated, may hold values from 0.3 to 0.6
- first_kernel: bfloat16 [3, 3, 96, 320], replicated, may hold values from -0.109375 to 0.109375
- second_kernel: bfloat16 [3, 3, 96, 96], replicated, may hold values from -0.21875 to 0.21875
- out_weight: bfloat16 [64, 96], replicated, may hold values from -0.625 to 0.625
Outputs:
- next_states: float32 [32, 64, 128, 256], P('tm', None, 'space')
The draws below stay inside these ranges and needn't reach their ends.
All inputs are finite; a program needn't handle non-finite values. No bound on the sum of `station_mask` on one device may be relied on, other than what follows from the above.
Results may differ from the reference program's by a relative error of at most 0.00054.
Values may be sent and summed in bfloat16 or wider, within the bound.
No kernel may reach another device: no remote copies, remote signals or barrier semaphores. Data moves between devices by JAX's collectives and lax.ppermute only.
A program may use at most 64 MiB of HBM per device.

```python
import jax
import jax.numpy as jnp
from jax import lax

C = 64
HID = 96
LON = 256
STATES = 32
LAT = 128


def touch_ends(entries, own_key, least, largest):
    extent = entries.shape
    spot = [jax.random.randint(jax.random.fold_in(own_key, axis), (), 0, extent[axis]) for axis in range(len(extent))]
    entries = entries.at[tuple(spot)].set(least)
    longest = extent.index(max(extent))
    spot[longest] = (spot[longest] + 1) % extent[longest]
    return entries.at[tuple(spot)].set(largest)


def level_of(rng, shape, cuts, low, largest):
    factor_of = 1.0
    for axis_at, parts in cuts:
        draws = jax.random.uniform(jax.random.fold_in(jax.random.fold_in(rng, 6), axis_at), (parts,), jnp.float32, low / len(cuts), largest / len(cuts))
        factor_of = factor_of * jnp.repeat(jnp.exp(draws), shape[axis_at] // parts).reshape((-1,) + (1,) * (len(shape) - 1 - axis_at))
    return factor_of


def centred(own_key, shape, deviation, limit, pieces=(), kind=jnp.bfloat16):
    values = jax.random.normal(own_key, shape, jnp.float32) * deviation
    if len(pieces) > 0:
        values = level_of(own_key, shape, pieces, -0.22, 0.18) * values
    return jnp.clip(values, min=-limit, max=limit).astype(kind)


def setup_inputs(seed: int = 0) -> dict:
    streams_of = jax.random.split(jax.random.key(seed), 10)
    states = centred(streams_of[0], (STATES, C, LAT, LON), 1.0, 6.0, ((0, 16), (2, 16)))
    observed = centred(streams_of[1], (STATES, C, LAT, LON), 1.0, 6.0, ((0, 16), (2, 16)))
    station_mask = touch_ends((jax.random.randint(streams_of[2], (STATES, LAT, LON), 0, 4) < 1).astype(jnp.int32), jax.random.fold_in(streams_of[2], 1), 0, 1)
    noise = centred(streams_of[3], (STATES, C, LAT, LON), 1.0, 6.0, ((0, 16), (2, 16)), jnp.float32)
    sigma_now = jnp.clip(jax.random.uniform(streams_of[4], (1,), jnp.float32, 0.8, 1.2), 0.8, 1.2)
    sigma_next = jnp.clip(jax.random.uniform(streams_of[5], (1,), jnp.float32, 0.3, 0.6), 0.3, 0.6)
    first_kernel = centred(streams_of[6], (3, 3, HID, 5 * C), (45 * C) ** -0.5, 0.109375)
    second_kernel = centred(streams_of[7], (3, 3, HID, HID), (9 * HID) ** -0.5, 0.21875)
    out_weight = centred(streams_of[8], (C, HID), HID ** -0.5, 0.625)
    return {"states": states, "observed": observed, "station_mask": station_mask, "noise": noise, "sigma_now": sigma_now, "sigma_next": sigma_next, "first_kernel": first_kernel, "second_kernel": second_kernel, "out_weight": out_weight}


def conv_layer(source, kernel, rows):
    total = jnp.zeros((kernel.shape[2], rows * LON), jnp.float32)
    for offa in range(3):
        for offb in range(3):
            piece = source[:, offa:offa + rows, offb:offb + LON].reshape(source.shape[0], rows * LON)
            total = total + jnp.dot(kernel[offa, offb], piece, preferred_element_type=jnp.float32)
    return total

def reference(states, observed, station_mask, noise, sigma_now, sigma_next, first_kernel, second_kernel, out_weight):
    level = sigma_now[0]
    later = sigma_next[0]
    scale_in = 1.0 / jnp.sqrt(1.0 + level * level)
    extended = jnp.pad(states, ((2, 2), (0, 0), (1, 1), (1, 1)))

    def one_state(index):
        window = lax.dynamic_slice_in_dim(extended, index, 5, 0)
        window = window.reshape(5 * C, LAT + 2, LON + 2)
        pre_one = conv_layer(window, first_kernel, LAT)
        hidden_one = jax.nn.silu(pre_one * scale_in).astype(jnp.bfloat16).reshape(HID, LAT, LON)
        padded = jnp.pad(hidden_one, ((0, 0), (1, 1), (1, 1)))
        pre_two = conv_layer(padded, second_kernel, LAT)
        hidden_two = jax.nn.silu(pre_two).astype(jnp.bfloat16)
        return jnp.dot(out_weight, hidden_two, preferred_element_type=jnp.float32).reshape(C, LAT, LON)
    estimate = lax.map(one_state, jnp.arange(STATES, dtype=jnp.int32))
    current = states.astype(jnp.float32)
    weight_obs = station_mask.astype(jnp.float32)[:, None, :, :]
    score = -estimate / level + weight_obs * (observed.astype(jnp.float32) - current) / (0.1 + level * level)
    drop = level * level - later * later
    return current + drop * score + jnp.sqrt(drop) * noise
```

```python
import functools

import jax
import jax.numpy as jnp
from jax import lax
from jax.experimental import pallas as pl
from jax.experimental.pallas import tpu as pltpu
from jax.sharding import PartitionSpec as P

F32 = jnp.float32
BF16 = jnp.bfloat16
AXES = ("tm", "space")
WID = 256
CH = 64
HID = 96


def core_swap(x, tm):
    return lax.ppermute(x, "tm", [(i, i ^ 1) for i in range(tm)])


def side_swap(x, tm):
    pairs = [(i, ((i + 1) ^ 1) - 1) for i in range(tm)]
    return lax.ppermute(x, "tm", [(i, j) for i, j in pairs if 0 <= j < tm])


def row_swap(x, tm, space):
    pairs = []
    for t in range(tm):
        step = -1 if t % 2 == 0 else 1
        for s in range(space):
            if 0 <= s + step < space:
                pairs.append((t * space + s, (t ^ 1) * space + s + step))
    return lax.ppermute(x, AXES, pairs)


def rows_first(states_ref, out_ref):
    n = states_ref.shape[0] * CH
    out_ref[...] = jnp.swapaxes(states_ref[...].reshape(n, states_ref.shape[2], WID), 0, 1)


def silu(v):
    u = 0.5 * v
    return u + u * jnp.tanh(u)


def side_shifts(v):
    lane = lax.broadcasted_iota(jnp.int32, v.shape, v.ndim - 1)
    right = jnp.where(lane == 0, 0.0, pltpu.roll(v, 1, v.ndim - 1))
    left = jnp.where(lane == WID - 1, 0.0, pltpu.roll(v, WID - 1, v.ndim - 1))
    return right, left


def put_shifted(dst, row, start, size, block):
    right, left = side_shifts(block.astype(F32))
    dst[row, 0, pl.ds(start, size)] = right.astype(BF16)
    dst[row, 1, pl.ds(start, size)] = block
    dst[row, 2, pl.ds(start, size)] = left.astype(BF16)


def step_kernel(
    place_ref,
    scalar_ref,
    own_ref,
    partner_ref,
    remote_ref,
    rows_a_ref,
    rows_b_ref,
    corner_ref,
    first_ref,
    second_ref,
    proj_ref,
    mask_ref,
    states_v,
    observed_v,
    noise_v,
    out_hbm,
    xs,
    w_one,
    w_two,
    hs,
    h2s,
    est,
    out_v,
    sems,
):
    core = place_ref[0]
    has_up = place_ref[1]
    has_down = place_ref[2]
    cur_k = scalar_ref[0]
    est_k = scalar_ref[1]
    obs_k = scalar_ref[2]
    noise_k = scalar_ref[3]
    scale_in = scalar_ref[4]

    for a in range(3):
        for b in range(3):
            n = a * 3 + b
            w_one[:, n * 5 * CH : (n + 1) * 5 * CH] = first_ref[a, b]
            w_two[:, n * HID : (n + 1) * HID] = second_ref[a, b]

    partner_at = pl.multiple_of((1 - core) * 4 * CH, 2 * CH)
    remote_at = pl.multiple_of(core * 4 * CH, 2 * CH)
    local_at = pl.multiple_of((1 - core) * 2 * CH, 2 * CH)
    for l in range(8):
        put_shifted(xs, l + 2, 2 * CH, 2 * CH, own_ref[l])
        put_shifted(xs, l + 2, partner_at, 2 * CH, partner_ref[l])
        put_shifted(xs, l + 2, remote_at, 2 * CH, remote_ref[l])
    for l in range(2):
        top = jnp.where(core == 0, rows_a_ref[l], rows_b_ref[l])
        low = jnp.where(core == 0, rows_b_ref[l], rows_a_ref[l])
        put_shifted(xs, l, local_at, 4 * CH, top)
        put_shifted(xs, l + 10, local_at, 4 * CH, low)
        put_shifted(xs, l, remote_at, 2 * CH, corner_ref[l])
        put_shifted(xs, l + 10, remote_at, 2 * CH, corner_ref[l + 2])

    for t in range(2):
        for r in range(10):
            window = jnp.concatenate(
                [xs[r + a, b, t * CH : (t + 5) * CH] for a in range(3) for b in range(3)], axis=0
            )
            pre = jnp.dot(w_one[...], window, preferred_element_type=F32)
            hid = silu(pre * scale_in)
            if r == 0:
                hid = jnp.where(has_up > 0, hid, 0.0)
            if r == 9:
                hid = jnp.where(has_down > 0, hid, 0.0)
            right, left = side_shifts(hid)
            hs[r, 0] = right.astype(BF16)
            hs[r, 1] = hid.astype(BF16)
            hs[r, 2] = left.astype(BF16)
        for r in range(8):
            pre = jnp.dot(
                w_two[...], hs[r : r + 3].reshape(9 * HID, WID), preferred_element_type=F32
            )
            h2s[r] = silu(pre).astype(BF16)
        for r in range(8):
            val = jnp.dot(proj_ref[...], h2s[r], preferred_element_type=F32)
            est[0, pl.ds(r, CH, stride=8), :] = val[:, :128]
            est[1, pl.ds(r, CH, stride=8), :] = val[:, 128:]
        weight = mask_ref[t].astype(F32) * obs_k
        estimate = jnp.concatenate([est[0], est[1]], axis=1).reshape(CH, 8, WID)
        current = states_v[t].astype(F32)
        seen = observed_v[t].astype(F32)
        out_v[t] = (
            current
            + est_k * estimate
            + weight[None] * (seen - current)
            + noise_k * noise_v[t]
        )
        pltpu.make_async_copy(out_v.at[t], out_hbm.at[t], sems.at[t]).start()
    for t in range(2):
        pltpu.make_async_copy(out_v.at[t], out_hbm.at[t], sems.at[t]).wait()


def body(
    states,
    observed,
    station_mask,
    noise,
    sigma_now,
    sigma_next,
    first_kernel,
    second_kernel,
    out_weight,
):
    tm, space = lax.axis_size("tm"), lax.axis_size("space")
    core = lax.axis_index("tm") % 2
    row_at = lax.axis_index("space")
    is_zero = core == 0
    vmem = pl.BlockSpec(memory_space=pltpu.VMEM)
    smem = pl.BlockSpec(memory_space=pltpu.SMEM)
    anywhere = pl.BlockSpec(memory_space=pl.ANY)

    own = pl.pallas_call(
        rows_first,
        out_shape=jax.ShapeDtypeStruct((8, 2 * CH, WID), BF16),
        in_specs=[vmem],
        out_specs=vmem,
        name="rows_first",
    )(states)

    top, foot = own[:2], own[6:]
    keep = jnp.where(is_zero, top, foot)
    give = jnp.where(is_zero, foot, top)
    got = core_swap(give, tm)
    edge = jnp.concatenate([jnp.where(is_zero, keep, got), jnp.where(is_zero, got, keep)], axis=1)
    rows_a = row_swap(edge, tm, space)
    own_late, rows_late = lax.optimization_barrier((own, edge))
    partner = core_swap(own_late, tm)
    remote = side_swap(own_late, tm)
    rows_b = core_swap(rows_a, tm)
    mine_a = jnp.where(is_zero, rows_a[:, : 2 * CH], rows_a[:, 2 * CH :])
    mine_b = jnp.where(is_zero, rows_b[:, : 2 * CH], rows_b[:, 2 * CH :])
    upper = jnp.where(is_zero, mine_a, mine_b)
    lower = jnp.where(is_zero, mine_b, mine_a)
    corner = side_swap(jnp.concatenate([upper, lower], axis=0), tm)

    level, later = sigma_now[0], sigma_next[0]
    drop = level * level - later * later
    scalars = jnp.stack(
        [
            level,
            -drop / level,
            drop / (0.1 + level * level),
            jnp.sqrt(drop),
            1.0 / jnp.sqrt(1.0 + level * level),
        ]
    )
    place = jnp.stack([core, row_at > 0, row_at < space - 1]).astype(jnp.int32)

    return pl.pallas_call(
        step_kernel,
        out_shape=jax.ShapeDtypeStruct(noise.shape, F32),
        in_specs=[smem] * 2 + [vmem] * 13,
        out_specs=anywhere,
        scratch_shapes=[
            pltpu.VMEM((12, 3, 6 * CH, WID), BF16),
            pltpu.VMEM((HID, 45 * CH), BF16),
            pltpu.VMEM((HID, 9 * HID), BF16),
            pltpu.VMEM((10, 3, HID, WID), BF16),
            pltpu.VMEM((8, HID, WID), BF16),
            pltpu.VMEM((2, CH * 8, 128), F32),
            pltpu.VMEM(noise.shape, F32),
            pltpu.SemaphoreType.DMA((2,)),
        ],
        compiler_params=pltpu.CompilerParams(vmem_limit_bytes=40 * 2**20),
        name="step",
    )(
        place,
        scalars,
        own,
        partner,
        remote,
        rows_a,
        rows_b,
        corner,
        first_kernel,
        second_kernel,
        out_weight,
        station_mask,
        states,
        observed,
        noise,
    )


def solution(mesh):
    in_specs = (
        P("tm", None, "space", None),
        P("tm", None, "space", None),
        P("tm", "space", None),
        P("tm", None, "space", None),
        P(),
        P(),
        P(),
        P(),
        P(),
    )
    out_specs = P("tm", None, "space", None)
    return jax.shard_map(body, mesh=mesh, in_specs=in_specs, out_specs=out_specs, check_vma=False)
```

```python
import jax
import jax.numpy as jnp
from jax import lax
from jax.experimental import pallas as pl
from jax.experimental.pallas import tpu as pltpu
from jax.sharding import PartitionSpec as P

F32 = jnp.float32
BF16 = jnp.bfloat16
AXES = ("tm", "space")
WID = 256
ROWS = 8
CH = 64
HID = 96
TWO = 2 * CH
FOUR = 4 * CH


def core_swap(x, tm):
    return lax.ppermute(x, "tm", [(i, i ^ 1) for i in range(tm)])


def side_swap(x, tm):
    pairs = [(i, ((i + 1) ^ 1) - 1) for i in range(tm)]
    return lax.ppermute(x, "tm", [(i, j) for i, j in pairs if 0 <= j < tm])


def row_swap(x, tm, space):
    pairs = []
    for t in range(tm):
        step = -1 if t % 2 == 0 else 1
        for s in range(space):
            if 0 <= s + step < space:
                pairs.append((t * space + s, (t ^ 1) * space + s + step))
    return lax.ppermute(x, AXES, pairs)


def core_of():
    return lax.axis_index("tm") % 2


def silu(v):
    u = 0.5 * v
    return u + u * jnp.tanh(u)


def dot(a, b):
    return jnp.dot(a, b, preferred_element_type=F32)


def side_shifts(v):
    lane = lax.broadcasted_iota(jnp.int32, v.shape, v.ndim - 1)
    right = jnp.where(lane == 0, 0.0, pltpu.roll(v, 1, v.ndim - 1))
    left = jnp.where(lane == WID - 1, 0.0, pltpu.roll(v, WID - 1, v.ndim - 1))
    return right, left


def put_shifted(dst, start, block):
    size = block.shape[0]
    wide = block.astype(F32)
    right, left = side_shifts(wide)
    dst[0, pl.ds(start, size)] = right.astype(BF16)
    dst[1, pl.ds(start, size)] = block.astype(BF16)
    dst[2, pl.ds(start, size)] = left.astype(BF16)


def scale_in(now_ref):
    level = jnp.full((8, WID), now_ref[0], F32)
    return (1.0 / jnp.sqrt(1.0 + level * level))[:1]


def hidden_two(row_of, w_two_ref, t, r):
    window = [row_of(r + a)[b, t * HID : (t + 1) * HID] for a in (-1, 0, 1) for b in range(3)]
    return silu(dot(w_two_ref[...], jnp.concatenate(window, axis=0))).astype(BF16)


def put_estimate(est, r, val):
    est[0, pl.ds(r, CH, stride=ROWS), :] = val[:, :128]
    est[1, pl.ds(r, CH, stride=ROWS), :] = val[:, 128:]


def estimate_of(est):
    return jnp.concatenate([est[0], est[1]], axis=1).reshape(CH, ROWS, WID)


def rows_first(block):
    return jnp.swapaxes(block.reshape(TWO, ROWS, WID), 0, 1)


def own_kernel(states_ref, own_ref, block_v, sems):
    parts = sems.shape[0]
    size = TWO // parts
    copies = []
    for n in range(parts):
        t, c = divmod(n * size, CH)
        copies.append(pltpu.make_async_copy(states_ref.at[t, pl.ds(c, size)], block_v.at[n], sems.at[n]))
        copies[-1].start()
    for n in range(parts):
        copies[n].wait()
        own_ref[:, n * size : (n + 1) * size] = jnp.swapaxes(block_v[n], 0, 1)


def edge_kernel(own_ref, partner_ref, edge_ref):
    core = core_of()
    far = rows_first(partner_ref[...])
    edge_ref[:, pl.ds(pl.multiple_of(core * TWO, TWO), TWO)] = own_ref[pl.ds(core * (ROWS - 2), 2)]
    edge_ref[:, pl.ds(pl.multiple_of((1 - core) * TWO, TWO), TWO)] = jnp.where(core == 0, far[:2], far[-2:])


def corner_kernel(rows_a_ref, rows_b_ref, send_ref):
    core = core_of()
    mine = pl.ds(pl.multiple_of(core * TWO, TWO), TWO)
    send_ref[pl.ds(core * 2, 2)] = rows_a_ref[:, mine]
    send_ref[pl.ds((1 - core) * 2, 2)] = rows_b_ref[:, mine]


def rim_or(rim, mid, l):
    return rim.at[l if l < 2 else l - 4] if l in (0, 1, 6, 7) else mid.at[l - 2]


def three_rows(rows):
    return jnp.concatenate([r[...].reshape(-1, WID) for r in rows], axis=0)


def near_kernel(
    own_ref,
    partner_ref,
    first_ref,
    second_ref,
    w_near_ref,
    w_far_ref,
    w_two_ref,
    rim_ref,
    part_ref,
    rows_v,
    mid,
    first_v,
    second_v,
    sems,
):
    first_copy = pltpu.make_async_copy(first_ref, first_v, sems.at[0])
    second_copy = pltpu.make_async_copy(second_ref, second_v, sems.at[1])
    first_copy.start()
    second_copy.start()
    core = core_of()
    own_at = pl.multiple_of(core * TWO, TWO)
    partner_at = pl.multiple_of((1 - core) * TWO, TWO)
    rows_v[...] = rows_first(partner_ref[...])
    for l in range(ROWS):
        put_shifted(rim_or(rim_ref, mid, l), own_at, own_ref[l])
        put_shifted(rim_or(rim_ref, mid, l), partner_at, rows_v[l])

    first_copy.wait()
    second_copy.wait()
    blank = jnp.zeros((HID, CH), BF16)
    for n in range(9):
        a, b = divmod(n, 3)
        block = first_v[a, b]
        for t, six in enumerate(([block, blank], [blank, block])):
            six = jnp.concatenate(six, axis=1)
            near = jnp.where(core == 0, six[:, TWO:], six[:, :FOUR])
            far = jnp.where(core == 0, six[:, :TWO], six[:, FOUR:])
            w_near_ref[t * HID : (t + 1) * HID, n * FOUR : (n + 1) * FOUR] = near
            w_far_ref[t * HID : (t + 1) * HID, n * TWO : (n + 1) * TWO] = far
        w_two_ref[:, n * HID : (n + 1) * HID] = second_v[a, b]
    for r in range(1, ROWS - 1):
        window = three_rows([rim_or(rim_ref, mid, r + a) for a in (-1, 0, 1)])
        part_ref[r - 1] = dot(w_near_ref[...], window)


def far_kernel(now_ref, remote_ref, part_ref, w_far_ref, rim_ref, hid_ref, rows_v, mid):
    scale = scale_in(now_ref)
    rows_v[...] = rows_first(remote_ref[...])
    for l in range(ROWS):
        put_shifted(rim_or(rim_ref, mid, l), 0, rows_v[l])
    for r in range(1, ROWS - 1):
        window = three_rows([rim_or(rim_ref, mid, r + a) for a in (-1, 0, 1)])
        pre = part_ref[r - 1] + dot(w_far_ref[...], window)
        put_shifted(hid_ref.at[r - 1], 0, silu(pre * scale))


def middle_kernel(
    now_ref,
    next_ref,
    hid_ref,
    w_two_ref,
    proj_ref,
    mask_ref,
    states_ref,
    observed_ref,
    noise_ref,
    base_ref,
    h2s,
    est,
):
    for t in range(2):
        for r in range(2, 6):
            h2s[t, r - 2] = hidden_two(lambda i: hid_ref.at[i - 1], w_two_ref, t, r)

    level = jnp.full((ROWS, WID), now_ref[0], F32)
    later = jnp.full((ROWS, WID), next_ref[0], F32)
    drop = level * level - later * later
    obs_k = drop / (0.1 + level * level)
    noise_k = jnp.sqrt(drop)
    est_k = -drop / level
    est[...] = jnp.zeros(est.shape, F32)
    for t in range(2):
        for r in range(2, 6):
            put_estimate(est, r, dot(proj_ref[...], h2s[t, r - 2]))
        weight = mask_ref[t].astype(F32) * obs_k
        current = states_ref[t].astype(F32)
        seen = observed_ref[t].astype(F32)
        base_ref[t] = (
            current
            + est_k[None] * estimate_of(est)
            + weight[None] * (seen - current)
            + noise_k[None] * noise_ref[t]
        )


def rim_kernel(rows_a_ref, rows_b_ref, near_ref, far_ref, w_near_ref, w_far_ref, part_ref, halo):
    core = core_of()
    for l in range(2):
        put_shifted(halo.at[l], 0, jnp.where(core == 0, rows_a_ref[l], rows_b_ref[l]))
        put_shifted(halo.at[l + 2], 0, jnp.where(core == 0, rows_b_ref[l], rows_a_ref[l]))

    def near(*rows):
        return dot(w_near_ref[...], three_rows(rows))

    def far(a, l, n):
        columns = slice(3 * a * TWO, 3 * (a + n) * TWO)
        return dot(w_far_ref[:, columns], far_ref[l : l + n].reshape(3 * n * TWO, WID))

    part_ref[0] = near(halo.at[0], halo.at[1], near_ref.at[0]) + far(2, 0, 1)
    part_ref[1] = near(halo.at[1], near_ref.at[0], near_ref.at[1]) + far(1, 0, 2)
    part_ref[2] = near(near_ref.at[2], near_ref.at[3], halo.at[2]) + far(0, 2, 2)
    part_ref[3] = near(near_ref.at[3], halo.at[2], halo.at[3]) + far(0, 3, 1)


def outer_kernel(
    now_ref,
    next_ref,
    corner_ref,
    part_ref,
    w_far_ref,
    w_two_ref,
    proj_ref,
    hid_ref,
    base_ref,
    out_ref,
    far,
    hrim,
    h2s,
    est,
    out_v,
    sems,
):
    for l in range(4):
        put_shifted(far.at[l], 0, corner_ref[l])
    scale = scale_in(now_ref)
    up = lax.axis_index("space") > 0
    down = lax.axis_index("space") < lax.axis_size("space") - 1

    def far_one(a, l):
        return dot(w_far_ref[:, 3 * a * TWO : 3 * (a + 1) * TWO], far[l].reshape(3 * TWO, WID))

    def far_two(a, l):
        return dot(w_far_ref[:, 3 * a * TWO : 3 * (a + 2) * TWO], far[l : l + 2].reshape(6 * TWO, WID))

    pre = [
        part_ref[0] + far_two(0, 0),
        part_ref[1] + far_one(0, 1),
        part_ref[2] + far_one(2, 2),
        part_ref[3] + far_two(1, 2),
    ]
    hid = [silu(p * scale) for p in pre]
    hid[0] = jnp.where(up, hid[0], 0.0)
    hid[3] = jnp.where(down, hid[3], 0.0)
    for l in range(4):
        put_shifted(hrim.at[l], 0, hid[l])

    def row(r):
        return hid_ref.at[r - 1] if 0 < r < ROWS - 1 else hrim.at[r + 1 if r < 1 else r - 5]

    edge = (0, 1, 6, 7)
    level = jnp.full((ROWS, WID), now_ref[0], F32)
    later = jnp.full((ROWS, WID), next_ref[0], F32)
    est_k = -(level * level - later * later) / level
    est[...] = jnp.zeros(est.shape, F32)
    for t in range(2):
        for n, r in enumerate(edge):
            h2s[t, n] = hidden_two(row, w_two_ref, t, r)
        for n, r in enumerate(edge):
            put_estimate(est.at[t], r, dot(proj_ref[...], h2s[t, n]))
        out_v[t] = base_ref[t] + est_k[None] * estimate_of(est.at[t])
        pltpu.make_async_copy(out_v.at[t], out_ref.at[t], sems.at[t]).start()
    for t in range(2):
        pltpu.make_async_copy(out_v.at[t], out_ref.at[t], sems.at[t]).wait()


VMEM = pl.BlockSpec(memory_space=pltpu.VMEM)
SMEM = pl.BlockSpec(memory_space=pltpu.SMEM)
ANY = pl.BlockSpec(memory_space=pl.ANY)
HBM = pl.BlockSpec(memory_space=pltpu.HBM)


def in_hbm(x):
    return pltpu.with_memory_space_constraint(x, pltpu.HBM)


def call(kernel, outs, ins, scratch=(), mib=4, flops=0, scalars=0, hbm=0, out_specs=None):
    shapes = [jax.ShapeDtypeStruct(s, d) for s, d in outs]
    return pl.pallas_call(
        kernel,
        out_shape=shapes,
        in_specs=[SMEM] * scalars + [VMEM] * (len(ins) - scalars - hbm) + [HBM] * hbm,
        out_specs=out_specs or [VMEM] * len(shapes),
        scratch_shapes=scratch,
        compiler_params=pltpu.CompilerParams(vmem_limit_bytes=mib * 2**20),
        cost_estimate=pl.CostEstimate(flops=flops, bytes_accessed=2**20, transcendentals=0),
        name=kernel.__name__,
    )(*ins)


def body(
    states,
    observed,
    station_mask,
    noise,
    sigma_now,
    sigma_next,
    first_kernel,
    second_kernel,
    out_weight,
):
    tm, space = lax.axis_size("tm"), lax.axis_size("space")
    partner = core_swap(states, tm)
    (own,) = call(
        own_kernel,
        [((ROWS, TWO, WID), BF16)],
        [in_hbm(states)],
        [pltpu.VMEM((4, TWO // 4, ROWS, WID), BF16), pltpu.SemaphoreType.DMA((4,))],
        hbm=1,
    )
    (edge,) = call(edge_kernel, [((2, FOUR, WID), BF16)], [own, partner])
    rows_a = row_swap(edge, tm, space)
    remote = side_swap(states, tm)
    w_near, w_far, w_two, near_rim, part = call(
        near_kernel,
        [
            ((2 * HID, 9 * FOUR), BF16),
            ((2 * HID, 9 * TWO), BF16),
            ((HID, 9 * HID), BF16),
            ((4, 3, FOUR, WID), BF16),
            ((6, 2 * HID, WID), F32),
        ],
        [own, partner, in_hbm(first_kernel), in_hbm(second_kernel)],
        [
            pltpu.VMEM((ROWS, TWO, WID), BF16),
            pltpu.VMEM((4, 3, FOUR, WID), BF16),
            pltpu.VMEM(first_kernel.shape, BF16),
            pltpu.VMEM(second_kernel.shape, BF16),
            pltpu.SemaphoreType.DMA((2,)),
        ],
        mib=16,
        flops=2 * 10**9,
        hbm=2,
    )
    far_rim, hid = call(
        far_kernel,
        [((4, 3, TWO, WID), BF16), ((6, 3, 2 * HID, WID), BF16)],
        [sigma_now, remote, part, w_far],
        [pltpu.VMEM((ROWS, TWO, WID), BF16), pltpu.VMEM((4, 3, TWO, WID), BF16)],
        mib=8,
        flops=10**9,
        scalars=1,
    )
    rows_a, hid, far_rim = lax.optimization_barrier((rows_a, hid, far_rim))
    rows_b = core_swap(rows_a, tm)
    (send,) = call(corner_kernel, [((4, TWO, WID), BF16)], [rows_a, rows_b])
    corner = side_swap(send, tm)
    (part,) = call(
        rim_kernel,
        [((4, 2 * HID, WID), F32)],
        [rows_a, rows_b, near_rim, far_rim, w_near, w_far],
        [pltpu.VMEM((4, 3, FOUR, WID), BF16)],
        mib=12,
        flops=10**9,
    )
    (base,) = call(
        middle_kernel,
        [(noise.shape, F32)],
        [
            sigma_now,
            sigma_next,
            hid,
            w_two,
            out_weight,
            station_mask,
            states,
            observed,
            noise,
        ],
        [pltpu.VMEM((2, 4, HID, WID), BF16), pltpu.VMEM((2, CH * ROWS, 128), F32)],
        mib=8,
        flops=10**9,
        scalars=2,
    )
    (out,) = call(
        outer_kernel,
        [(noise.shape, F32)],
        [sigma_now, sigma_next, corner, part, w_far, w_two, out_weight, hid, base],
        [
            pltpu.VMEM((4, 3, TWO, WID), BF16),
            pltpu.VMEM((4, 3, 2 * HID, WID), BF16),
            pltpu.VMEM((2, 4, HID, WID), BF16),
            pltpu.VMEM((2, 2, CH * ROWS, 128), F32),
            pltpu.VMEM(noise.shape, F32),
            pltpu.SemaphoreType.DMA((2,)),
        ],
        mib=12,
        flops=10**9,
        scalars=2,
        out_specs=[ANY],
    )
    return out


def solution(mesh):
    in_specs = (
        P("tm", None, "space", None),
        P("tm", None, "space", None),
        P("tm", "space", None),
        P("tm", None, "space", None),
        P(),
        P(),
        P(),
        P(),
        P(),
    )
    out_specs = P("tm", None, "space", None)
    return jax.shard_map(body, mesh=mesh, in_specs=in_specs, out_specs=out_specs, check_vma=False)
```

```python
import jax
import jax.numpy as jnp
from jax import lax
from jax.experimental import pallas as pl
from jax.experimental.pallas import tpu as pltpu
from jax.sharding import PartitionSpec as P

F32 = jnp.float32
BF16 = jnp.bfloat16
AXES = ("tm", "space")
WID = 256
ROWS = 8
CH = 64
HID = 96
TWO = 2 * CH
FOUR = 4 * CH


def core_swap(x, tm):
    return lax.ppermute(x, "tm", [(i, i ^ 1) for i in range(tm)])


def side_swap(x, tm):
    return lax.ppermute(x, "tm", [(i, (((i + 1) ^ 1) - 1) % tm) for i in range(tm)])


def most_swap(x, tm):
    pairs = [(i, ((i + 1) ^ 1) - 1) for i in range(tm)]
    return lax.ppermute(x, "tm", [(i, j) for i, j in pairs if 0 <= j < tm and i + j != tm - 1])


def middle_swap(x, tm):
    low = tm // 2 - 1
    return lax.ppermute(x, "tm", [(low, low + 1), (low + 1, low)])


def row_swap(x, tm, space):
    pairs = []
    for t in range(tm):
        step = -1 if t % 2 == 0 else 1
        for s in range(space):
            inside = 0 <= s + step < space
            pairs.append((t * space + s, (t ^ 1) * space + s + step if inside else (t ^ 2) * space + s))
    return lax.ppermute(x, AXES, pairs)


def core_of():
    return lax.axis_index("tm") % 2


def silu(v):
    u = 0.5 * v
    return u + u * jnp.tanh(u)


def dot(a, b):
    return jnp.dot(a, b, preferred_element_type=F32)


def rows_first(block):
    return jnp.swapaxes(block.reshape(TWO, ROWS, WID), 0, 1)


def side_shifts(v):
    lane = lax.broadcasted_iota(jnp.int32, v.shape, v.ndim - 1)
    zero = jnp.zeros((), v.dtype)
    right = jnp.where(lane == 0, zero, pltpu.roll(v, 1, v.ndim - 1))
    left = jnp.where(lane == WID - 1, zero, pltpu.roll(v, WID - 1, v.ndim - 1))
    return right, left


def put_sides(dst, start, block):
    right, left = side_shifts(block)
    dst[0, pl.ds(start, block.shape[0])] = right
    dst[1, pl.ds(start, block.shape[0])] = left


def stacked(sides, *centre):
    return jnp.concatenate([sides[0], *centre, sides[1]], axis=0)


def put_hidden(dst, hid):
    right, left = side_shifts(hid)
    dst[0] = right.astype(BF16)
    dst[1] = hid.astype(BF16)
    dst[2] = left.astype(BF16)


def two_rows(row_of, w_two_ref, t, r):
    window = [row_of(i)[b, t * HID : (t + 1) * HID] for i in range(r - 1, r + 3) for b in range(3)]
    return silu(dot(w_two_ref[...], jnp.concatenate(window, axis=0))).astype(BF16)


def put_estimates(est, r, val):
    for n in range(2):
        est[0, pl.ds(r + n, CH, stride=ROWS), :] = val[n * CH : (n + 1) * CH, :128]
        est[1, pl.ds(r + n, CH, stride=ROWS), :] = val[n * CH : (n + 1) * CH, 128:]


def prepare_kernel(
    states_ref,
    first_ref,
    second_ref,
    proj_ref,
    own_ref,
    w_near_ref,
    w_far_ref,
    w_two_ref,
    w_proj_ref,
    block_v,
    first_v,
    second_v,
    proj_v,
    sems,
):
    parts = block_v.shape[0]
    size = TWO // parts
    copies = []
    for n in range(parts):
        t, c = divmod(n * size, CH)
        copies.append(pltpu.make_async_copy(states_ref.at[t, pl.ds(c, size)], block_v.at[n], sems.at[n]))
    copies += [
        pltpu.make_async_copy(first_ref, first_v, sems.at[parts]),
        pltpu.make_async_copy(second_ref, second_v, sems.at[parts + 1]),
        pltpu.make_async_copy(proj_ref, proj_v, sems.at[parts + 2]),
    ]
    for copy in copies:
        copy.start()
    core = core_of()
    for n in range(parts):
        copies[n].wait()
        own_ref[:, n * size : (n + 1) * size] = jnp.swapaxes(block_v[n], 0, 1)
    for copy in copies[parts:]:
        copy.wait()
    blank = jnp.zeros((HID, CH), BF16)
    for n in range(9):
        block = first_v[n // 3, n % 3]
        for t, six in enumerate(([block, blank], [blank, block])):
            six = jnp.concatenate(six, axis=1)
            first, last = six[:, :TWO], six[:, FOUR:]
            rows = slice(t * HID, (t + 1) * HID)
            w_near_ref[rows, n * FOUR : n * FOUR + TWO] = six[:, TWO:FOUR]
            w_near_ref[rows, n * FOUR + TWO : (n + 1) * FOUR] = jnp.where(core == 0, last, first)
            w_far_ref[rows, n * TWO : (n + 1) * TWO] = jnp.where(core == 0, first, last)
    blank = jnp.zeros((HID, 3 * HID), BF16)
    w_two_ref[:HID, 9 * HID :] = blank
    w_two_ref[HID:, : 3 * HID] = blank
    for n in range(9):
        block = second_v[n // 3, n % 3]
        w_two_ref[:HID, n * HID : (n + 1) * HID] = block
        w_two_ref[HID:, (n + 3) * HID : (n + 4) * HID] = block
    blank = jnp.zeros((CH, HID), BF16)
    w_proj_ref[:CH] = jnp.concatenate([proj_v[...], blank], axis=1)
    w_proj_ref[CH:] = jnp.concatenate([blank, proj_v[...]], axis=1)


def edge_kernel(own_ref, partner_ref, edge_ref):
    core = core_of()
    other = rows_first(partner_ref[...])
    last = jnp.where(core == 0, 0, lax.axis_size("space") - 1)
    inside = lax.axis_index("space") != last
    zero = jnp.zeros((), BF16)
    mine = jnp.where(inside, own_ref[pl.ds(core * (ROWS - 2), 2)], zero)
    other = jnp.where(inside, jnp.where(core == 0, other[:2], other[-2:]), zero)
    edge_ref[:, pl.ds(pl.multiple_of(core * TWO, TWO), TWO)] = mine
    edge_ref[:, pl.ds(pl.multiple_of((1 - core) * TWO, TWO), TWO)] = other


def at_end():
    at = lax.axis_index("tm")
    return (at == 0) | (at == lax.axis_size("tm") - 1)


def corner_kernel(rows_a_ref, rows_b_ref, send_ref):
    core = core_of()
    mine = pl.ds(pl.multiple_of(core * TWO, TWO), TWO)
    zero = jnp.zeros((), BF16)
    send_ref[pl.ds(core * 2, 2)] = jnp.where(at_end(), zero, rows_a_ref[:, mine])
    send_ref[pl.ds((1 - core) * 2, 2)] = jnp.where(at_end(), zero, rows_b_ref[:, mine])


def rim_or(rim, mid, l):
    return rim.at[l if l < 2 else l - 4] if l in (0, 1, 6, 7) else mid.at[l - 2]


def near_kernel(own_ref, partner_ref, w_near_ref, partner_rows_ref, rim_ref, part_ref, mid):
    partner_rows_ref[...] = rows_first(partner_ref[...])

    def shift_row(l):
        put_sides(rim_or(rim_ref, mid, l), 0, own_ref[l])
        put_sides(rim_or(rim_ref, mid, l), TWO, partner_rows_ref[l])

    def row(l):
        return stacked(rim_or(rim_ref, mid, l), own_ref[l], partner_rows_ref[l])

    for l in range(3):
        shift_row(l)
    for r in range(1, ROWS - 1):
        if r + 2 < ROWS:
            shift_row(r + 2)
        window = jnp.concatenate([row(r + a) for a in (-1, 0, 1)], axis=0)
        part_ref[r - 1] = dot(w_near_ref[...], window)


def base_kernel(
    now_ref, next_ref, mask_ref, states_ref, observed_ref, noise_ref, base_ref, coef_ref
):
    level = jnp.full((ROWS, WID), now_ref[0], F32)
    later = jnp.full((ROWS, WID), next_ref[0], F32)
    drop = level * level - later * later
    coef_ref[0] = 1.0 / jnp.sqrt(1.0 + level * level)
    coef_ref[1] = -drop / level
    obs_k = drop / (0.1 + level * level)
    noise_k = jnp.sqrt(drop)
    for t in range(2):
        weight = mask_ref[t].astype(F32) * obs_k
        current = states_ref[t].astype(F32)
        seen = observed_ref[t].astype(F32)
        base_ref[t] = current + weight[None] * (seen - current) + noise_k[None] * noise_ref[t]


def rim_kernel(
    rows_a_ref, rows_b_ref, own_ref, partner_rows_ref, near_ref, w_near_ref, part_ref, halo, sides
):
    core = core_of()
    own_at = pl.multiple_of(core * TWO, TWO)
    partner_at = pl.multiple_of((1 - core) * TWO, TWO)
    for l in range(2):
        for n, at in ((0, own_at), (1, partner_at)):
            a, b = rows_a_ref[l, pl.ds(at, TWO)], rows_b_ref[l, pl.ds(at, TWO)]
            halo[l, n * TWO : (n + 1) * TWO] = jnp.where(core == 0, a, b)
            halo[l + 2, n * TWO : (n + 1) * TWO] = jnp.where(core == 0, b, a)

    def tile(l):
        return stacked(near_ref.at[l if l < 2 else l - 4], own_ref[l], partner_rows_ref[l])

    def outside(l):
        put_sides(sides.at[l], 0, halo[l])
        return stacked(sides.at[l], halo[l])

    def near(*rows):
        return dot(w_near_ref[...], jnp.concatenate(rows, axis=0))

    above, below = [outside(0), outside(1)], [outside(2), outside(3)]
    part_ref[0] = near(above[0], above[1], tile(0))
    part_ref[1] = near(above[1], tile(0), tile(1))
    part_ref[2] = near(tile(6), tile(7), below[0])
    part_ref[3] = near(tile(7), below[0], below[1])


def far_kernel(
    most_ref, middle_ref, part_ref, rim_part_ref, w_far_ref, coef_ref, hid_ref, rim_out_ref, rows_v, sides
):
    scale = coef_ref[0][:1]
    at, size = lax.axis_index("tm"), lax.axis_size("tm")
    in_middle = (at == size // 2 - 1) | (at == size // 2)
    block = jnp.where(in_middle, middle_ref[...], most_ref[...])
    rows_v[...] = rows_first(jnp.where(at_end(), jnp.zeros((), BF16), block))

    def far(a, l, n):
        columns = slice(3 * a * TWO, 3 * (a + n) * TWO)
        rows = [stacked(sides.at[i], rows_v[i]) for i in range(l, l + n)]
        return dot(w_far_ref[:, columns], jnp.concatenate(rows, axis=0))

    for l in range(3):
        put_sides(sides.at[l], 0, rows_v[l])
    for r in range(1, ROWS - 1):
        if r + 2 < ROWS:
            put_sides(sides.at[r + 2], 0, rows_v[r + 2])
        pre = part_ref[r - 1] + far(0, r - 1, 3)
        put_hidden(hid_ref.at[r - 1], silu(pre * scale))
    rim_out_ref[0] = rim_part_ref[0] + far(2, 0, 1)
    rim_out_ref[1] = rim_part_ref[1] + far(1, 0, 2)
    rim_out_ref[2] = rim_part_ref[2] + far(0, ROWS - 2, 2)
    rim_out_ref[3] = rim_part_ref[3] + far(0, ROWS - 1, 1)


def middle_kernel(hid_ref, w_two_ref, proj_ref, est_ref, h2s):
    spots = [(t, r) for t in range(2) for r in (2, 4)]
    for n, (t, r) in enumerate(spots):
        h2s[n] = two_rows(lambda i: hid_ref.at[i - 1], w_two_ref, t, r)
    for n, (t, r) in enumerate(spots):
        put_estimates(est_ref.at[t], r, dot(proj_ref[...], h2s[n]))


def outer_kernel(
    corner_ref,
    part_ref,
    w_far_ref,
    w_two_ref,
    proj_ref,
    coef_ref,
    hid_ref,
    base_ref,
    est_in_ref,
    out_ref,
    sides,
    hrim,
    h2s,
    est,
    out_v,
    sems,
):
    for l in range(4):
        put_sides(sides.at[l], 0, corner_ref[l])
    scale = coef_ref[0][:1]
    up = lax.axis_index("space") > 0
    down = lax.axis_index("space") < lax.axis_size("space") - 1

    def far(a, l, n):
        columns = slice(3 * a * TWO, 3 * (a + n) * TWO)
        rows = [stacked(sides.at[i], corner_ref[i]) for i in range(l, l + n)]
        return dot(w_far_ref[:, columns], jnp.concatenate(rows, axis=0))

    pre = [
        part_ref[0] + far(0, 0, 2),
        part_ref[1] + far(0, 1, 1),
        part_ref[2] + far(2, 2, 1),
        part_ref[3] + far(1, 2, 2),
    ]
    hid = [silu(p * scale) for p in pre]
    hid[0] = jnp.where(up, hid[0], 0.0)
    hid[3] = jnp.where(down, hid[3], 0.0)
    for l in range(4):
        put_hidden(hrim.at[l], hid[l])

    def row(r):
        return hid_ref.at[r - 1] if 0 < r < ROWS - 1 else hrim.at[r + 1 if r < 1 else r - 5]

    est[...] = est_in_ref[...]
    half = CH // 2
    copies = []
    for t in range(2):
        for n, r in enumerate((0, 6)):
            h2s[t, n] = two_rows(row, w_two_ref, t, r)
        for n, r in enumerate((0, 6)):
            put_estimates(est.at[t], r, dot(proj_ref[...], h2s[t, n]))
        for n in range(2):
            channels = slice(n * half, (n + 1) * half)
            rows = slice(n * half * ROWS, (n + 1) * half * ROWS)
            val = jnp.concatenate([est[t, 0, rows], est[t, 1, rows]], axis=1).reshape(half, ROWS, WID)
            out_v[t, channels] = base_ref[t, channels] + coef_ref[1][None] * val
            at = (t, pl.ds(n * half, half))
            copies.append(pltpu.make_async_copy(out_v.at[at], out_ref.at[at], sems.at[2 * t + n]))
            copies[-1].start()
    for copy in copies:
        copy.wait()


VMEM = pl.BlockSpec(memory_space=pltpu.VMEM)
SMEM = pl.BlockSpec(memory_space=pltpu.SMEM)
ANY = pl.BlockSpec(memory_space=pl.ANY)
HBM = pl.BlockSpec(memory_space=pltpu.HBM)


def in_hbm(x):
    return pltpu.with_memory_space_constraint(x, pltpu.HBM)


def call(kernel, outs, ins, scratch=(), mib=4, flops=0, scalars=0, hbm=0, out_specs=None):
    shapes = [jax.ShapeDtypeStruct(s, d) for s, d in outs]
    ins = list(ins[: len(ins) - hbm]) + [in_hbm(x) for x in ins[len(ins) - hbm :]]
    return pl.pallas_call(
        kernel,
        out_shape=shapes,
        in_specs=[SMEM] * scalars + [VMEM] * (len(ins) - scalars - hbm) + [HBM] * hbm,
        out_specs=out_specs or [VMEM] * len(shapes),
        scratch_shapes=scratch,
        compiler_params=pltpu.CompilerParams(vmem_limit_bytes=mib * 2**20),
        cost_estimate=pl.CostEstimate(flops=flops, bytes_accessed=2**20, transcendentals=0),
        name=kernel.__name__,
    )(*ins)


def body(
    states,
    observed,
    station_mask,
    noise,
    sigma_now,
    sigma_next,
    first_kernel,
    second_kernel,
    out_weight,
):
    tm, space = lax.axis_size("tm"), lax.axis_size("space")
    rows_shape = ((ROWS, TWO, WID), BF16)
    partner = core_swap(states, tm)
    own, w_near, w_far, w_two, w_proj = call(
        prepare_kernel,
        [
            rows_shape,
            ((2 * HID, 9 * FOUR), BF16),
            ((2 * HID, 9 * TWO), BF16),
            ((2 * HID, 12 * HID), BF16),
            ((2 * CH, 2 * HID), BF16),
        ],
        [states, first_kernel, second_kernel, out_weight],
        [
            pltpu.VMEM((4, TWO // 4, ROWS, WID), BF16),
            pltpu.VMEM(first_kernel.shape, BF16),
            pltpu.VMEM(second_kernel.shape, BF16),
            pltpu.VMEM(out_weight.shape, BF16),
            pltpu.SemaphoreType.DMA((7,)),
        ],
        mib=8,
        hbm=4,
    )
    (edge,) = call(edge_kernel, [((2, FOUR, WID), BF16)], [own, partner])
    edge, states_x = lax.optimization_barrier((edge, states))
    rows_a = row_swap(edge, tm, space)
    most = most_swap(states_x, tm)
    partner_rows, near_rim, part = call(
        near_kernel,
        [rows_shape, ((4, 2, FOUR, WID), BF16), ((6, 2 * HID, WID), F32)],
        [own, partner, w_near],
        [pltpu.VMEM((4, 2, FOUR, WID), BF16)],
        mib=16,
        flops=2 * 10**9,
    )
    states_late, part = lax.optimization_barrier((states, part))
    middle = middle_swap(states_late, tm)
    rows_a, part = lax.optimization_barrier((rows_a, part))
    rows_b = core_swap(rows_a, tm)
    (send,) = call(corner_kernel, [((4, TWO, WID), BF16)], [rows_a, rows_b])
    send, noise_late = lax.optimization_barrier((send, noise))
    base, coef = call(
        base_kernel,
        [(noise.shape, F32), ((2, ROWS, WID), F32)],
        [sigma_now, sigma_next, station_mask, states, observed, noise_late],
        flops=10**8,
        scalars=2,
    )
    corner = side_swap(send, tm)
    (rim_part,) = call(
        rim_kernel,
        [((4, 2 * HID, WID), F32)],
        [rows_a, rows_b, own, partner_rows, near_rim, w_near],
        [pltpu.VMEM((4, FOUR, WID), BF16), pltpu.VMEM((4, 2, FOUR, WID), BF16)],
        mib=12,
        flops=10**9,
    )
    hid, rim_part = call(
        far_kernel,
        [((6, 3, 2 * HID, WID), BF16), ((4, 2 * HID, WID), F32)],
        [most, middle, part, rim_part, w_far, coef],
        [pltpu.VMEM((ROWS, TWO, WID), BF16), pltpu.VMEM((ROWS, 2, TWO, WID), BF16)],
        mib=8,
        flops=10**9,
    )
    (est,) = call(
        middle_kernel,
        [((2, 2, CH * ROWS, 128), F32)],
        [hid, w_two, w_proj],
        [pltpu.VMEM((4, 2 * HID, WID), BF16)],
        mib=8,
        flops=10**9,
    )
    (out,) = call(
        outer_kernel,
        [(noise.shape, F32)],
        [corner, rim_part, w_far, w_two, w_proj, coef, hid, base, est],
        [
            pltpu.VMEM((4, 2, TWO, WID), BF16),
            pltpu.VMEM((4, 3, 2 * HID, WID), BF16),
            pltpu.VMEM((2, 2, 2 * HID, WID), BF16),
            pltpu.VMEM((2, 2, CH * ROWS, 128), F32),
            pltpu.VMEM(noise.shape, F32),
            pltpu.SemaphoreType.DMA((4,)),
        ],
        mib=12,
        flops=10**9,
        out_specs=[ANY],
    )
    return out


def solution(mesh):
    in_specs = (
        P("tm", None, "space", None),
        P("tm", None, "space", None),
        P("tm", "space", None),
        P("tm", None, "space", None),
        P(),
        P(),
        P(),
        P(),
        P(),
    )
    out_specs = P("tm", None, "space", None)
    return jax.shard_map(body, mesh=mesh, in_specs=in_specs, out_specs=out_specs, check_vma=False)
```

```python
import jax
import jax.numpy as jnp
from jax import lax
from jax.experimental import pallas as pl
from jax.experimental.pallas import tpu as pltpu
from jax.sharding import PartitionSpec as P

F32 = jnp.float32
BF16 = jnp.bfloat16
AXES = ("tm", "space")
WID = 256
ROWS = 8
CH = 64
HID = 96
TWO = 2 * CH
FOUR = 4 * CH


def core_swap(x, tm):
    return lax.ppermute(x, "tm", [(i, i ^ 1) for i in range(tm)])


def side_swap(x, tm):
    return lax.ppermute(x, "tm", [(i, (((i + 1) ^ 1) - 1) % tm) for i in range(tm)])


def most_swap(x, tm):
    pairs = [(i, ((i + 1) ^ 1) - 1) for i in range(tm)]
    return lax.ppermute(x, "tm", [(i, j) for i, j in pairs if 0 <= j < tm and i + j != tm - 1])


def middle_swap(x, tm):
    low = tm // 2 - 1
    return lax.ppermute(x, "tm", [(low, low + 1), (low + 1, low)])


def row_swap(x, tm, space):
    pairs = []
    for t in range(tm):
        step = -1 if t % 2 == 0 else 1
        for s in range(space):
            inside = 0 <= s + step < space
            pairs.append((t * space + s, (t ^ 1) * space + s + step if inside else (t ^ 2) * space + s))
    return lax.ppermute(x, AXES, pairs)


def core_of():
    return lax.axis_index("tm") % 2


def silu(v):
    u = 0.5 * v
    return u + u * jnp.tanh(u)


def dot(a, b):
    return jnp.dot(a, b, preferred_element_type=F32)


def rows_first(block):
    return jnp.swapaxes(block.reshape(TWO, ROWS, WID), 0, 1)


def side_shifts(v):
    lane = lax.broadcasted_iota(jnp.int32, v.shape, v.ndim - 1)
    zero = jnp.zeros((), v.dtype)
    right = jnp.where(lane == 0, zero, pltpu.roll(v, 1, v.ndim - 1))
    left = jnp.where(lane == WID - 1, zero, pltpu.roll(v, WID - 1, v.ndim - 1))
    return right, left


def put_sides(dst, start, block):
    right, left = side_shifts(block)
    dst[0, pl.ds(start, block.shape[0])] = right
    dst[1, pl.ds(start, block.shape[0])] = left


def stacked(sides, *centre):
    return jnp.concatenate([sides[0], *centre, sides[1]], axis=0)


def put_hidden(dst, hid):
    hid = hid.astype(BF16)
    dst[0], dst[2] = side_shifts(hid)
    dst[1] = hid


def hidden_window(row_of, t, rows):
    return jnp.concatenate([row_of(i)[b, t * HID : (t + 1) * HID] for i in rows for b in range(3)], axis=0)


def add_estimates(acc, est_k, r, val):
    val = est_k * val
    for half in range(2):
        flat = acc.at[half].reshape(CH * ROWS, 128)
        for n in range(2):
            rows = pl.ds(r + n, CH, stride=ROWS)
            flat[rows, :] = flat[rows, :] + val[n * CH : (n + 1) * CH, half * 128 : (half + 1) * 128]


def prepare_kernel(
    states_ref,
    first_ref,
    second_ref,
    proj_ref,
    own_ref,
    w_near_ref,
    w_far_ref,
    w_two_ref,
    w_proj_ref,
    block_v,
    first_v,
    second_v,
    proj_v,
    sems,
):
    parts = block_v.shape[0]
    size = TWO // parts
    copies = []
    for n in range(parts):
        t, c = divmod(n * size, CH)
        copies.append(pltpu.make_async_copy(states_ref.at[t, pl.ds(c, size)], block_v.at[n], sems.at[n]))
    copies += [
        pltpu.make_async_copy(first_ref, first_v, sems.at[parts]),
        pltpu.make_async_copy(second_ref, second_v, sems.at[parts + 1]),
        pltpu.make_async_copy(proj_ref, proj_v, sems.at[parts + 2]),
    ]
    for copy in copies:
        copy.start()
    core = core_of()
    for n in range(parts):
        copies[n].wait()
        own_ref[:, n * size : (n + 1) * size] = jnp.swapaxes(block_v[n], 0, 1)
    for copy in copies[parts:]:
        copy.wait()
    blank = jnp.zeros((HID, CH), BF16)
    for n in range(9):
        block = first_v[n // 3, n % 3]
        for t, six in enumerate(([block, blank], [blank, block])):
            six = jnp.concatenate(six, axis=1)
            first, last = six[:, :TWO], six[:, FOUR:]
            rows = slice(t * HID, (t + 1) * HID)
            w_near_ref[rows, n * FOUR : n * FOUR + TWO] = six[:, TWO:FOUR]
            w_near_ref[rows, n * FOUR + TWO : (n + 1) * FOUR] = jnp.where(core == 0, last, first)
            w_far_ref[rows, n * TWO : (n + 1) * TWO] = jnp.where(core == 0, first, last)
    blank = jnp.zeros((HID, 3 * HID), BF16)
    w_two_ref[:HID, 9 * HID :] = blank
    w_two_ref[HID:, : 3 * HID] = blank
    for n in range(9):
        block = second_v[n // 3, n % 3]
        w_two_ref[:HID, n * HID : (n + 1) * HID] = block
        w_two_ref[HID:, (n + 3) * HID : (n + 4) * HID] = block
    blank = jnp.zeros((CH, HID), BF16)
    w_proj_ref[:CH] = jnp.concatenate([proj_v[...], blank], axis=1)
    w_proj_ref[CH:] = jnp.concatenate([blank, proj_v[...]], axis=1)


def edge_kernel(own_ref, partner_ref, edge_ref):
    core = core_of()
    other = rows_first(partner_ref[...])
    last = jnp.where(core == 0, 0, lax.axis_size("space") - 1)
    inside = lax.axis_index("space") != last
    zero = jnp.zeros((), BF16)
    mine = jnp.where(inside, own_ref[pl.ds(core * (ROWS - 2), 2)], zero)
    other = jnp.where(inside, jnp.where(core == 0, other[:2], other[-2:]), zero)
    edge_ref[:, pl.ds(pl.multiple_of(core * TWO, TWO), TWO)] = mine
    edge_ref[:, pl.ds(pl.multiple_of((1 - core) * TWO, TWO), TWO)] = other


def at_end():
    at = lax.axis_index("tm")
    return (at == 0) | (at == lax.axis_size("tm") - 1)


def corner_kernel(rows_a_ref, rows_b_ref, send_ref):
    core = core_of()
    mine = pl.ds(pl.multiple_of(core * TWO, TWO), TWO)
    zero = jnp.zeros((), BF16)
    send_ref[pl.ds(core * 2, 2)] = jnp.where(at_end(), zero, rows_a_ref[:, mine])
    send_ref[pl.ds((1 - core) * 2, 2)] = jnp.where(at_end(), zero, rows_b_ref[:, mine])


def near_rows(sides_ref, own_ref, partner_rows_ref, *rows):
    return jnp.concatenate([stacked(sides_ref.at[l], own_ref[l], partner_rows_ref[l]) for l in rows], axis=0)


def near_kernel(own_ref, partner_ref, w_near_ref, partner_rows_ref, sides_ref, part_ref, edge_part_ref):
    partner_rows_ref[...] = rows_first(partner_ref[...])
    for l in range(ROWS):
        put_sides(sides_ref.at[l], 0, own_ref[l])
        put_sides(sides_ref.at[l], TWO, partner_rows_ref[l])
        if 2 <= l < part_ref.shape[0] + 2:
            part_ref[l - 2] = dot(w_near_ref[...], near_rows(sides_ref, own_ref, partner_rows_ref, l - 2, l - 1, l))
        if l == 1:
            edge_part_ref[0] = dot(w_near_ref[:, 3 * FOUR :], near_rows(sides_ref, own_ref, partner_rows_ref, 0, 1))
    edge_part_ref[1] = dot(w_near_ref[:, : 6 * FOUR], near_rows(sides_ref, own_ref, partner_rows_ref, 6, 7))
    edge_part_ref[2] = dot(w_near_ref[:, : 3 * FOUR], near_rows(sides_ref, own_ref, partner_rows_ref, 7))


def rest_kernel(own_ref, partner_rows_ref, sides_ref, w_near_ref, part_ref):
    count = part_ref.shape[0]
    for n in range(count):
        r = ROWS - 1 - count + n
        window = near_rows(sides_ref, own_ref, partner_rows_ref, r - 1, r, r + 1)
        part_ref[n] = dot(w_near_ref[...], window)


def base_kernel(
    now_ref, next_ref, mask_ref, states_ref, observed_ref, noise_ref, base_ref, coef_ref
):
    level = jnp.full((ROWS, WID), now_ref[0], F32)
    later = jnp.full((ROWS, WID), next_ref[0], F32)
    drop = level * level - later * later
    coef_ref[0] = 1.0 / jnp.sqrt(1.0 + level * level)
    coef_ref[1] = -drop / level
    obs_k = drop / (0.1 + level * level)
    noise_k = jnp.sqrt(drop)
    for t in range(2):
        weight = mask_ref[t].astype(F32) * obs_k
        current = states_ref[t].astype(F32)
        seen = observed_ref[t].astype(F32)
        val = current + weight[None] * (seen - current) + noise_k[None] * noise_ref[t]
        base_ref[t, 0] = val[:, :, :128]
        base_ref[t, 1] = val[:, :, 128:]


def rim_kernel(
    rows_a_ref, rows_b_ref, own_ref, partner_rows_ref, near_ref, w_near_ref, edge_part_ref, part_ref, halo, sides
):
    core = core_of()
    own_at = pl.multiple_of(core * TWO, TWO)
    partner_at = pl.multiple_of((1 - core) * TWO, TWO)
    for l in range(2):
        for n, at in ((0, own_at), (1, partner_at)):
            a, b = rows_a_ref[l, pl.ds(at, TWO)], rows_b_ref[l, pl.ds(at, TWO)]
            halo[l, n * TWO : (n + 1) * TWO] = jnp.where(core == 0, a, b)
            halo[l + 2, n * TWO : (n + 1) * TWO] = jnp.where(core == 0, b, a)

    def tile(l):
        return stacked(near_ref.at[l], own_ref[l], partner_rows_ref[l])

    def outside(l):
        put_sides(sides.at[l], 0, halo[l])
        return stacked(sides.at[l], halo[l])

    def near(*rows):
        return dot(w_near_ref[...], jnp.concatenate(rows, axis=0))

    above, below = [outside(0), outside(1)], [outside(2), outside(3)]
    part_ref[0] = near(above[0], above[1], tile(0))
    part_ref[1] = edge_part_ref[0] + dot(w_near_ref[:, : 3 * FOUR], above[1])
    part_ref[2] = edge_part_ref[1] + dot(w_near_ref[:, 6 * FOUR :], below[0])
    part_ref[3] = edge_part_ref[2] + dot(w_near_ref[:, 3 * FOUR :], jnp.concatenate(below, axis=0))


def far_kernel(
    most_ref, middle_ref, part_ref, part_late_ref, rim_part_ref, w_far_ref, coef_ref, hid_ref, rim_out_ref, rows_v, sides
):
    scale = coef_ref[0][:1]
    at, size = lax.axis_index("tm"), lax.axis_size("tm")
    in_middle = (at == size // 2 - 1) | (at == size // 2)
    block = jnp.where(in_middle, middle_ref[...], most_ref[...])
    rows_v[...] = rows_first(jnp.where(at_end(), jnp.zeros((), BF16), block))

    def far(a, l, n):
        columns = slice(3 * a * TWO, 3 * (a + n) * TWO)
        rows = [stacked(sides.at[i], rows_v[i]) for i in range(l, l + n)]
        return dot(w_far_ref[:, columns], jnp.concatenate(rows, axis=0))

    for l in range(3):
        put_sides(sides.at[l], 0, rows_v[l])
    for r in range(1, ROWS - 1):
        if r + 2 < ROWS:
            put_sides(sides.at[r + 2], 0, rows_v[r + 2])
        early = part_ref.shape[0]
        part = part_ref[r - 1] if r <= early else part_late_ref[r - 1 - early]
        pre = part + far(0, r - 1, 3)
        put_hidden(hid_ref.at[r - 1], silu(pre * scale))
    rim_out_ref[0] = rim_part_ref[0] + far(2, 0, 1)
    rim_out_ref[1] = rim_part_ref[1] + far(1, 0, 2)
    rim_out_ref[2] = rim_part_ref[2] + far(0, ROWS - 2, 2)
    rim_out_ref[3] = rim_part_ref[3] + far(0, ROWS - 1, 1)


def middle_kernel(hid_ref, w_two_ref, proj_ref, coef_ref, base_ref, known_ref, acc_ref, h2s):
    est_k = coef_ref[1][:1]

    def row(r):
        return hid_ref.at[r - 1]

    spots = [(t, r) for t in range(2) for r in (2, 4)]
    for n, (t, r) in enumerate(spots):
        window = hidden_window(row, t, range(r - 1, r + 3))
        h2s[n] = silu(dot(w_two_ref[...], window)).astype(BF16)
    for t in range(2):
        known_ref[t, 0] = dot(w_two_ref[:, 6 * HID :], hidden_window(row, t, (1, 2)))
        known_ref[t, 1] = dot(w_two_ref[:, : 6 * HID], hidden_window(row, t, (ROWS - 3, ROWS - 2)))
    for n, (t, r) in enumerate(spots):
        add_estimates(acc_ref.at[t], est_k, r, dot(proj_ref[...], h2s[n]))


def outer_kernel(
    corner_ref,
    part_ref,
    w_far_ref,
    w_two_ref,
    proj_ref,
    coef_ref,
    known_ref,
    base_ref,
    out_ref,
    acc_ref,
    sides,
    hrim,
    h2s,
    sems,
):
    for l in range(4):
        put_sides(sides.at[l], 0, corner_ref[l])
    scale = coef_ref[0][:1]
    up = lax.axis_index("space") > 0
    down = lax.axis_index("space") < lax.axis_size("space") - 1

    def far(a, l, n):
        columns = slice(3 * a * TWO, 3 * (a + n) * TWO)
        rows = [stacked(sides.at[i], corner_ref[i]) for i in range(l, l + n)]
        return dot(w_far_ref[:, columns], jnp.concatenate(rows, axis=0))

    pre = [
        part_ref[0] + far(0, 0, 2),
        part_ref[1] + far(0, 1, 1),
        part_ref[2] + far(2, 2, 1),
        part_ref[3] + far(1, 2, 2),
    ]
    hid = [silu(p * scale) for p in pre]
    hid[0] = jnp.where(up, hid[0], 0.0)
    hid[3] = jnp.where(down, hid[3], 0.0)
    for l in range(4):
        put_hidden(hrim.at[l], hid[l])

    est_k = coef_ref[1][:1]
    spots = [(t, n) for n in range(2) for t in range(2)]
    weights = (w_two_ref[:, : 6 * HID], w_two_ref[:, 6 * HID :])
    for t, n in spots:
        window = hidden_window(lambda i: hrim.at[i], t, (2 * n, 2 * n + 1))
        h2s[t, n] = silu(known_ref[t, n] + dot(weights[n], window)).astype(BF16)
    for t, n in spots:
        add_estimates(acc_ref.at[t], est_k, n * (ROWS - 2), dot(proj_ref[...], h2s[t, n]))
    copies = []
    for t, half in spots:
        target = out_ref.at[t, :, :, pl.ds(half * 128, 128)]
        copies.append(pltpu.make_async_copy(acc_ref.at[t, half], target, sems.at[2 * t + half]))
        copies[-1].start()
    for copy in copies:
        copy.wait()


VMEM = pl.BlockSpec(memory_space=pltpu.VMEM)
SMEM = pl.BlockSpec(memory_space=pltpu.SMEM)
ANY = pl.BlockSpec(memory_space=pl.ANY)
HBM = pl.BlockSpec(memory_space=pltpu.HBM)


def in_hbm(x):
    return pltpu.with_memory_space_constraint(x, pltpu.HBM)


def call(kernel, outs, ins, scratch=(), mib=4, flops=0, scalars=0, hbm=0, out_specs=None, alias=()):
    shapes = [jax.ShapeDtypeStruct(s, d) for s, d in outs]
    ins = list(ins[: len(ins) - hbm]) + [in_hbm(x) for x in ins[len(ins) - hbm :]]
    return pl.pallas_call(
        kernel,
        out_shape=shapes,
        in_specs=[SMEM] * scalars + [VMEM] * (len(ins) - scalars - hbm) + [HBM] * hbm,
        out_specs=out_specs or [VMEM] * len(shapes),
        scratch_shapes=scratch,
        input_output_aliases=dict(alias),
        compiler_params=pltpu.CompilerParams(vmem_limit_bytes=mib * 2**20),
        cost_estimate=pl.CostEstimate(flops=flops, bytes_accessed=2**20, transcendentals=0),
        name=kernel.__name__,
    )(*ins)


def body(
    states,
    observed,
    station_mask,
    noise,
    sigma_now,
    sigma_next,
    first_kernel,
    second_kernel,
    out_weight,
):
    tm, space = lax.axis_size("tm"), lax.axis_size("space")
    rows_shape = ((ROWS, TWO, WID), BF16)
    acc_shape = ((2, 2, CH, ROWS, 128), F32)
    partner = core_swap(states, tm)
    own, w_near, w_far, w_two, w_proj = call(
        prepare_kernel,
        [
            rows_shape,
            ((2 * HID, 9 * FOUR), BF16),
            ((2 * HID, 9 * TWO), BF16),
            ((2 * HID, 12 * HID), BF16),
            ((2 * CH, 2 * HID), BF16),
        ],
        [states, first_kernel, second_kernel, out_weight],
        [
            pltpu.VMEM((4, TWO // 4, ROWS, WID), BF16),
            pltpu.VMEM(first_kernel.shape, BF16),
            pltpu.VMEM(second_kernel.shape, BF16),
            pltpu.VMEM(out_weight.shape, BF16),
            pltpu.SemaphoreType.DMA((7,)),
        ],
        mib=8,
        hbm=4,
    )
    (edge,) = call(edge_kernel, [((2, FOUR, WID), BF16)], [own, partner])
    edge, states_x = lax.optimization_barrier((edge, states))
    rows_a = row_swap(edge, tm, space)
    most = most_swap(states_x, tm)
    early = 5
    partner_rows, near_sides, part, edge_part = call(
        near_kernel,
        [rows_shape, ((ROWS, 2, FOUR, WID), BF16), ((early, 2 * HID, WID), F32), ((3, 2 * HID, WID), F32)],
        [own, partner, w_near],
        mib=8,
        flops=2 * 10**9,
    )
    states_late, part = lax.optimization_barrier((states, part))
    middle = middle_swap(states_late, tm)
    (part_late,) = call(
        rest_kernel,
        [((ROWS - 2 - early, 2 * HID, WID), F32)],
        [own, partner_rows, near_sides, w_near],
        mib=8,
    )
    rows_a, part, part_late = lax.optimization_barrier((rows_a, part, part_late))
    rows_b = core_swap(rows_a, tm)
    (send,) = call(corner_kernel, [((4, TWO, WID), BF16)], [rows_a, rows_b])
    send, noise_late = lax.optimization_barrier((send, noise))
    base, coef = call(
        base_kernel,
        [acc_shape, ((2, ROWS, WID), F32)],
        [sigma_now, sigma_next, station_mask, states, observed, noise_late],
        flops=10**8,
        scalars=2,
    )
    corner = side_swap(send, tm)
    (rim_part,) = call(
        rim_kernel,
        [((4, 2 * HID, WID), F32)],
        [rows_a, rows_b, own, partner_rows, near_sides, w_near, edge_part],
        [pltpu.VMEM((4, FOUR, WID), BF16), pltpu.VMEM((4, 2, FOUR, WID), BF16)],
        mib=12,
        flops=10**9,
    )
    hid, rim_part = call(
        far_kernel,
        [((6, 3, 2 * HID, WID), BF16), ((4, 2 * HID, WID), F32)],
        [most, middle, part, part_late, rim_part, w_far, coef],
        [pltpu.VMEM((ROWS, TWO, WID), BF16), pltpu.VMEM((ROWS, 2, TWO, WID), BF16)],
        mib=8,
        flops=10**9,
    )
    known, acc = call(
        middle_kernel,
        [((2, 2, 2 * HID, WID), F32), acc_shape],
        [hid, w_two, w_proj, coef, base],
        [pltpu.VMEM((4, 2 * HID, WID), BF16)],
        mib=8,
        flops=10**9,
        alias=[(4, 1)],
    )
    out, _ = call(
        outer_kernel,
        [(noise.shape, F32), acc_shape],
        [corner, rim_part, w_far, w_two, w_proj, coef, known, acc],
        [
            pltpu.VMEM((4, 2, TWO, WID), BF16),
            pltpu.VMEM((4, 3, 2 * HID, WID), BF16),
            pltpu.VMEM((2, 2, 2 * HID, WID), BF16),
            pltpu.SemaphoreType.DMA((4,)),
        ],
        mib=12,
        flops=10**9,
        out_specs=[ANY, VMEM],
        alias=[(7, 1)],
    )
    return out


def solution(mesh):
    in_specs = (
        P("tm", None, "space", None),
        P("tm", None, "space", None),
        P("tm", "space", None),
        P("tm", None, "space", None),
        P(),
        P(),
        P(),
        P(),
        P(),
    )
    out_specs = P("tm", None, "space", None)
    return jax.shard_map(body, mesh=mesh, in_specs=in_specs, out_specs=out_specs, check_vma=False)
```

```python
import jax
import jax.numpy as jnp
from jax import lax
from jax.experimental import pallas as pl
from jax.experimental.pallas import tpu as pltpu
from jax.sharding import PartitionSpec as P

F32 = jnp.float32
BF16 = jnp.bfloat16
AXES = ("tm", "space")
WID = 256
ROWS = 8
CH = 64
HID = 96
TWO = 2 * CH
FOUR = 4 * CH


def core_swap(x, tm):
    return lax.ppermute(x, "tm", [(i, i ^ 1) for i in range(tm)])


def side_swap(x, tm):
    return lax.ppermute(x, "tm", [(i, (((i + 1) ^ 1) - 1) % tm) for i in range(tm)])


def most_swap(x, tm):
    pairs = [(i, ((i + 1) ^ 1) - 1) for i in range(tm)]
    return lax.ppermute(x, "tm", [(i, j) for i, j in pairs if 0 <= j < tm and i + j != tm - 1])


def middle_swap(x, tm):
    low = tm // 2 - 1
    return lax.ppermute(x, "tm", [(low, low + 1), (low + 1, low)])


def row_swap(x, tm, space):
    pairs = []
    for t in range(tm):
        step = -1 if t % 2 == 0 else 1
        for s in range(space):
            inside = 0 <= s + step < space
            pairs.append((t * space + s, (t ^ 1) * space + s + step if inside else (t ^ 2) * space + s))
    return lax.ppermute(x, AXES, pairs)


def core_of():
    return lax.axis_index("tm") % 2


def silu(v):
    u = 0.5 * v
    return u + u * jnp.tanh(u)


def dot(a, b):
    return jnp.dot(a, b, preferred_element_type=F32)


def rows_first(block):
    return jnp.swapaxes(block.reshape(TWO, ROWS, WID), 0, 1)


def side_shifts(v):
    lane = lax.broadcasted_iota(jnp.int32, v.shape, v.ndim - 1)
    zero = jnp.zeros((), v.dtype)
    right = jnp.where(lane == 0, zero, pltpu.roll(v, 1, v.ndim - 1))
    left = jnp.where(lane == WID - 1, zero, pltpu.roll(v, WID - 1, v.ndim - 1))
    return right, left


def put_sides(dst, start, block):
    right, left = side_shifts(block)
    dst[0, pl.ds(start, block.shape[0])] = right
    dst[1, pl.ds(start, block.shape[0])] = left


def stacked(sides, *centre):
    return jnp.concatenate([sides[0], *centre, sides[1]], axis=0)


def put_hidden(dst, hid):
    hid = hid.astype(BF16)
    dst[0], dst[2] = side_shifts(hid)
    dst[1] = hid


def hidden_window(row_of, t, rows):
    return jnp.concatenate([row_of(i)[b, t * HID : (t + 1) * HID] for i in rows for b in range(3)], axis=0)


def add_estimates(acc, est_k, r, val):
    val = est_k * val
    for half in range(2):
        flat = acc.at[half].reshape(CH * ROWS, 128)
        for n in range(2):
            rows = pl.ds(r + n, CH, stride=ROWS)
            flat[rows, :] = flat[rows, :] + val[n * CH : (n + 1) * CH, half * 128 : (half + 1) * 128]


def prepare_kernel(
    states_ref,
    first_ref,
    second_ref,
    proj_ref,
    own_ref,
    w_near_ref,
    w_far_ref,
    w_two_ref,
    w_proj_ref,
    block_v,
    first_v,
    second_v,
    proj_v,
    sems,
):
    parts = block_v.shape[0]
    size = TWO // parts
    copies = []
    for n in range(parts):
        t, c = divmod(n * size, CH)
        copies.append(pltpu.make_async_copy(states_ref.at[t, pl.ds(c, size)], block_v.at[n], sems.at[n]))
    copies += [
        pltpu.make_async_copy(first_ref, first_v, sems.at[parts]),
        pltpu.make_async_copy(second_ref, second_v, sems.at[parts + 1]),
        pltpu.make_async_copy(proj_ref, proj_v, sems.at[parts + 2]),
    ]
    for copy in copies:
        copy.start()
    core = core_of()
    for n in range(parts):
        copies[n].wait()
        own_ref[:, n * size : (n + 1) * size] = jnp.swapaxes(block_v[n], 0, 1)
    for copy in copies[parts:]:
        copy.wait()
    blank = jnp.zeros((HID, CH), BF16)
    for n in range(9):
        block = first_v[n // 3, n % 3]
        for t, six in enumerate(([block, blank], [blank, block])):
            six = jnp.concatenate(six, axis=1)
            first, last = six[:, :TWO], six[:, FOUR:]
            rows = slice(t * HID, (t + 1) * HID)
            w_near_ref[rows, n * FOUR : n * FOUR + TWO] = six[:, TWO:FOUR]
            w_near_ref[rows, n * FOUR + TWO : (n + 1) * FOUR] = jnp.where(core == 0, last, first)
            w_far_ref[rows, n * TWO : (n + 1) * TWO] = jnp.where(core == 0, first, last)
    blank = jnp.zeros((HID, 3 * HID), BF16)
    w_two_ref[:HID, 9 * HID :] = blank
    w_two_ref[HID:, : 3 * HID] = blank
    for n in range(9):
        block = second_v[n // 3, n % 3]
        w_two_ref[:HID, n * HID : (n + 1) * HID] = block
        w_two_ref[HID:, (n + 3) * HID : (n + 4) * HID] = block
    blank = jnp.zeros((CH, HID), BF16)
    w_proj_ref[:CH] = jnp.concatenate([proj_v[...], blank], axis=1)
    w_proj_ref[CH:] = jnp.concatenate([blank, proj_v[...]], axis=1)


def edge_kernel(own_ref, partner_ref, edge_ref):
    core = core_of()
    other = rows_first(partner_ref[...])
    last = jnp.where(core == 0, 0, lax.axis_size("space") - 1)
    inside = lax.axis_index("space") != last
    zero = jnp.zeros((), BF16)
    mine = jnp.where(inside, own_ref[pl.ds(core * (ROWS - 2), 2)], zero)
    other = jnp.where(inside, jnp.where(core == 0, other[:2], other[-2:]), zero)
    edge_ref[:, pl.ds(pl.multiple_of(core * TWO, TWO), TWO)] = mine
    edge_ref[:, pl.ds(pl.multiple_of((1 - core) * TWO, TWO), TWO)] = other


def at_end():
    at = lax.axis_index("tm")
    return (at == 0) | (at == lax.axis_size("tm") - 1)


def corner_kernel(rows_a_ref, rows_b_ref, send_ref):
    core = core_of()
    mine = pl.ds(pl.multiple_of(core * TWO, TWO), TWO)
    zero = jnp.zeros((), BF16)
    send_ref[pl.ds(core * 2, 2)] = jnp.where(at_end(), zero, rows_a_ref[:, mine])
    send_ref[pl.ds((1 - core) * 2, 2)] = jnp.where(at_end(), zero, rows_b_ref[:, mine])


def near_rows(sides_ref, own_ref, partner_rows_ref, *rows):
    return jnp.concatenate([stacked(sides_ref.at[l], own_ref[l], partner_rows_ref[l]) for l in rows], axis=0)


def near_kernel(own_ref, partner_ref, w_near_ref, partner_rows_ref, sides_ref, part_ref, edge_part_ref):
    partner_rows_ref[...] = rows_first(partner_ref[...])
    for l in range(ROWS):
        put_sides(sides_ref.at[l], 0, own_ref[l])
        put_sides(sides_ref.at[l], TWO, partner_rows_ref[l])
        if 2 <= l < part_ref.shape[0] + 2:
            part_ref[l - 2] = dot(w_near_ref[...], near_rows(sides_ref, own_ref, partner_rows_ref, l - 2, l - 1, l))
        if l == 1:
            edge_part_ref[0] = dot(w_near_ref[:, 3 * FOUR :], near_rows(sides_ref, own_ref, partner_rows_ref, 0, 1))
    edge_part_ref[1] = dot(w_near_ref[:, : 6 * FOUR], near_rows(sides_ref, own_ref, partner_rows_ref, 6, 7))


def rest_kernel(own_ref, partner_rows_ref, sides_ref, w_near_ref, part_ref):
    count = part_ref.shape[0]
    for n in range(count):
        r = ROWS - 1 - count + n
        window = near_rows(sides_ref, own_ref, partner_rows_ref, r - 1, r, r + 1)
        part_ref[n] = dot(w_near_ref[...], window)


def base_kernel(
    now_ref, next_ref, mask_ref, states_ref, observed_ref, noise_ref, base_ref, coef_ref
):
    level = jnp.full((ROWS, WID), now_ref[0], F32)
    later = jnp.full((ROWS, WID), next_ref[0], F32)
    drop = level * level - later * later
    coef_ref[0] = 1.0 / jnp.sqrt(1.0 + level * level)
    coef_ref[1] = -drop / level
    obs_k = drop / (0.1 + level * level)
    noise_k = jnp.sqrt(drop)
    for t in range(2):
        weight = mask_ref[t].astype(F32) * obs_k
        current = states_ref[t].astype(F32)
        seen = observed_ref[t].astype(F32)
        val = current + weight[None] * (seen - current) + noise_k[None] * noise_ref[t]
        base_ref[t, 0] = val[:, :, :128]
        base_ref[t, 1] = val[:, :, 128:]


def rim_kernel(
    rows_a_ref, rows_b_ref, own_ref, partner_rows_ref, near_ref, w_near_ref, edge_part_ref, part_ref, halo, sides
):
    core = core_of()
    own_at = pl.multiple_of(core * TWO, TWO)
    partner_at = pl.multiple_of((1 - core) * TWO, TWO)
    for l in range(2):
        for n, at in ((0, own_at), (1, partner_at)):
            a, b = rows_a_ref[l, pl.ds(at, TWO)], rows_b_ref[l, pl.ds(at, TWO)]
            halo[l, n * TWO : (n + 1) * TWO] = jnp.where(core == 0, a, b)
            halo[l + 2, n * TWO : (n + 1) * TWO] = jnp.where(core == 0, b, a)

    def tile(l):
        return stacked(near_ref.at[l], own_ref[l], partner_rows_ref[l])

    def outside(l):
        put_sides(sides.at[l], 0, halo[l])
        return stacked(sides.at[l], halo[l])

    def near(*rows):
        return dot(w_near_ref[...], jnp.concatenate(rows, axis=0))

    above, below = [outside(0), outside(1)], [outside(2), outside(3)]
    part_ref[0] = near(above[0], above[1], tile(0))
    part_ref[1] = edge_part_ref[0] + dot(w_near_ref[:, : 3 * FOUR], above[1])
    part_ref[2] = edge_part_ref[1] + dot(w_near_ref[:, 6 * FOUR :], below[0])
    part_ref[3] = near(tile(7), below[0], below[1])


def far_kernel(
    most_ref, middle_ref, part_ref, part_late_ref, rim_part_ref, w_far_ref, coef_ref, hid_ref, rim_out_ref, rows_v, sides
):
    scale = coef_ref[0][:1]
    at, size = lax.axis_index("tm"), lax.axis_size("tm")
    in_middle = (at == size // 2 - 1) | (at == size // 2)
    block = jnp.where(in_middle, middle_ref[...], most_ref[...])
    rows_v[...] = rows_first(jnp.where(at_end(), jnp.zeros((), BF16), block))

    def far(a, l, n):
        columns = slice(3 * a * TWO, 3 * (a + n) * TWO)
        rows = [stacked(sides.at[i], rows_v[i]) for i in range(l, l + n)]
        return dot(w_far_ref[:, columns], jnp.concatenate(rows, axis=0))

    for l in range(3):
        put_sides(sides.at[l], 0, rows_v[l])
    for r in range(1, ROWS - 1):
        if r + 2 < ROWS:
            put_sides(sides.at[r + 2], 0, rows_v[r + 2])
        early = part_ref.shape[0]
        part = part_ref[r - 1] if r <= early else part_late_ref[r - 1 - early]
        pre = part + far(0, r - 1, 3)
        put_hidden(hid_ref.at[r - 1], silu(pre * scale))
    rim_out_ref[0] = rim_part_ref[0] + far(2, 0, 1)
    rim_out_ref[1] = rim_part_ref[1] + far(1, 0, 2)
    rim_out_ref[2] = rim_part_ref[2] + far(0, ROWS - 2, 2)
    rim_out_ref[3] = rim_part_ref[3] + far(0, ROWS - 1, 1)


def middle_kernel(hid_ref, w_two_ref, proj_ref, coef_ref, base_ref, known_ref, acc_ref, h2s):
    est_k = coef_ref[1][:1]

    def row(r):
        return hid_ref.at[r - 1]

    spots = [(t, r) for t in range(2) for r in (2, 4)]
    for n, (t, r) in enumerate(spots):
        window = hidden_window(row, t, range(r - 1, r + 3))
        h2s[n] = silu(dot(w_two_ref[...], window)).astype(BF16)
    for t in range(2):
        known_ref[t, 0] = dot(w_two_ref[:, 6 * HID :], hidden_window(row, t, (1, 2)))
        known_ref[t, 1] = dot(w_two_ref[:, : 6 * HID], hidden_window(row, t, (ROWS - 3, ROWS - 2)))
    for n, (t, r) in enumerate(spots):
        add_estimates(acc_ref.at[t], est_k, r, dot(proj_ref[...], h2s[n]))


def outer_kernel(
    corner_ref,
    part_ref,
    w_far_ref,
    w_two_ref,
    proj_ref,
    coef_ref,
    known_ref,
    base_ref,
    out_ref,
    acc_ref,
    sides,
    hrim,
    h2s,
    sems,
):
    for l in range(4):
        put_sides(sides.at[l], 0, corner_ref[l])
    scale = coef_ref[0][:1]
    up = lax.axis_index("space") > 0
    down = lax.axis_index("space") < lax.axis_size("space") - 1

    def far(a, l, n):
        columns = slice(3 * a * TWO, 3 * (a + n) * TWO)
        rows = [stacked(sides.at[i], corner_ref[i]) for i in range(l, l + n)]
        return dot(w_far_ref[:, columns], jnp.concatenate(rows, axis=0))

    pre = [
        part_ref[0] + far(0, 0, 2),
        part_ref[1] + far(0, 1, 1),
        part_ref[2] + far(2, 2, 1),
        part_ref[3] + far(1, 2, 2),
    ]
    hid = [silu(p * scale) for p in pre]
    hid[0] = jnp.where(up, hid[0], 0.0)
    hid[3] = jnp.where(down, hid[3], 0.0)
    for l in range(4):
        put_hidden(hrim.at[l], hid[l])

    est_k = coef_ref[1][:1]
    spots = [(t, n) for n in range(2) for t in range(2)]
    weights = (w_two_ref[:, : 6 * HID], w_two_ref[:, 6 * HID :])
    for t, n in spots:
        window = hidden_window(lambda i: hrim.at[i], t, (2 * n, 2 * n + 1))
        h2s[t, n] = silu(known_ref[t, n] + dot(weights[n], window)).astype(BF16)
    vals = {(t, n): dot(proj_ref[...], h2s[t, n]) for t, n in spots}
    copies = []
    for t in range(2):
        for n in range(2):
            add_estimates(acc_ref.at[t], est_k, n * (ROWS - 2), vals[t, n])
        for half in range(2):
            target = out_ref.at[t, :, :, pl.ds(half * 128, 128)]
            copies.append(pltpu.make_async_copy(acc_ref.at[t, half], target, sems.at[2 * t + half]))
            copies[-1].start()
    for copy in copies:
        copy.wait()


VMEM = pl.BlockSpec(memory_space=pltpu.VMEM)
SMEM = pl.BlockSpec(memory_space=pltpu.SMEM)
ANY = pl.BlockSpec(memory_space=pl.ANY)
HBM = pl.BlockSpec(memory_space=pltpu.HBM)


def in_hbm(x):
    return pltpu.with_memory_space_constraint(x, pltpu.HBM)


def call(kernel, outs, ins, scratch=(), mib=4, flops=0, scalars=0, hbm=0, out_specs=None, alias=()):
    shapes = [jax.ShapeDtypeStruct(s, d) for s, d in outs]
    ins = list(ins[: len(ins) - hbm]) + [in_hbm(x) for x in ins[len(ins) - hbm :]]
    return pl.pallas_call(
        kernel,
        out_shape=shapes,
        in_specs=[SMEM] * scalars + [VMEM] * (len(ins) - scalars - hbm) + [HBM] * hbm,
        out_specs=out_specs or [VMEM] * len(shapes),
        scratch_shapes=scratch,
        input_output_aliases=dict(alias),
        compiler_params=pltpu.CompilerParams(vmem_limit_bytes=mib * 2**20),
        cost_estimate=pl.CostEstimate(flops=flops, bytes_accessed=2**20, transcendentals=0),
        name=kernel.__name__,
    )(*ins)


def body(
    states,
    observed,
    station_mask,
    noise,
    sigma_now,
    sigma_next,
    first_kernel,
    second_kernel,
    out_weight,
):
    tm, space = lax.axis_size("tm"), lax.axis_size("space")
    rows_shape = ((ROWS, TWO, WID), BF16)
    acc_shape = ((2, 2, CH, ROWS, 128), F32)
    partner = core_swap(states, tm)
    own, w_near, w_far, w_two, w_proj = call(
        prepare_kernel,
        [
            rows_shape,
            ((2 * HID, 9 * FOUR), BF16),
            ((2 * HID, 9 * TWO), BF16),
            ((2 * HID, 12 * HID), BF16),
            ((2 * CH, 2 * HID), BF16),
        ],
        [states, first_kernel, second_kernel, out_weight],
        [
            pltpu.VMEM((4, TWO // 4, ROWS, WID), BF16),
            pltpu.VMEM(first_kernel.shape, BF16),
            pltpu.VMEM(second_kernel.shape, BF16),
            pltpu.VMEM(out_weight.shape, BF16),
            pltpu.SemaphoreType.DMA((7,)),
        ],
        mib=8,
        hbm=4,
    )
    (edge,) = call(edge_kernel, [((2, FOUR, WID), BF16)], [own, partner])
    edge, states_x = lax.optimization_barrier((edge, states))
    rows_a = row_swap(edge, tm, space)
    most = most_swap(states_x, tm)
    early = 5
    partner_rows, near_sides, part, edge_part = call(
        near_kernel,
        [rows_shape, ((ROWS, 2, FOUR, WID), BF16), ((early, 2 * HID, WID), F32), ((2, 2 * HID, WID), F32)],
        [own, partner, w_near],
        mib=8,
        flops=2 * 10**9,
    )
    states_late, part = lax.optimization_barrier((states, part))
    middle = middle_swap(states_late, tm)
    (part_late,) = call(
        rest_kernel,
        [((ROWS - 2 - early, 2 * HID, WID), F32)],
        [own, partner_rows, near_sides, w_near],
        mib=8,
    )
    rows_a, part, part_late = lax.optimization_barrier((rows_a, part, part_late))
    rows_b = core_swap(rows_a, tm)
    (send,) = call(corner_kernel, [((4, TWO, WID), BF16)], [rows_a, rows_b])
    send, noise_late = lax.optimization_barrier((send, noise))
    base, coef = call(
        base_kernel,
        [acc_shape, ((2, ROWS, WID), F32)],
        [sigma_now, sigma_next, station_mask, states, observed, noise_late],
        flops=10**8,
        scalars=2,
    )
    corner = side_swap(send, tm)
    (rim_part,) = call(
        rim_kernel,
        [((4, 2 * HID, WID), F32)],
        [rows_a, rows_b, own, partner_rows, near_sides, w_near, edge_part],
        [pltpu.VMEM((4, FOUR, WID), BF16), pltpu.VMEM((4, 2, FOUR, WID), BF16)],
        mib=12,
        flops=10**9,
    )
    hid, rim_part = call(
        far_kernel,
        [((6, 3, 2 * HID, WID), BF16), ((4, 2 * HID, WID), F32)],
        [most, middle, part, part_late, rim_part, w_far, coef],
        [pltpu.VMEM((ROWS, TWO, WID), BF16), pltpu.VMEM((ROWS, 2, TWO, WID), BF16)],
        mib=8,
        flops=10**9,
    )
    known, acc = call(
        middle_kernel,
        [((2, 2, 2 * HID, WID), F32), acc_shape],
        [hid, w_two, w_proj, coef, base],
        [pltpu.VMEM((4, 2 * HID, WID), BF16)],
        mib=8,
        flops=10**9,
        alias=[(4, 1)],
    )
    out, _ = call(
        outer_kernel,
        [(noise.shape, F32), acc_shape],
        [corner, rim_part, w_far, w_two, w_proj, coef, known, acc],
        [
            pltpu.VMEM((4, 2, TWO, WID), BF16),
            pltpu.VMEM((4, 3, 2 * HID, WID), BF16),
            pltpu.VMEM((2, 2, 2 * HID, WID), BF16),
            pltpu.SemaphoreType.DMA((4,)),
        ],
        mib=12,
        flops=10**9,
        out_specs=[ANY, VMEM],
        alias=[(7, 1)],
    )
    return out


def solution(mesh):
    in_specs = (
        P("tm", None, "space", None),
        P("tm", None, "space", None),
        P("tm", "space", None),
        P("tm", None, "space", None),
        P(),
        P(),
        P(),
        P(),
        P(),
    )
    out_specs = P("tm", None, "space", None)
    return jax.shard_map(body, mesh=mesh, in_specs=in_specs, out_specs=out_specs, check_vma=False)
```

```python
import jax
import jax.numpy as jnp
from jax import lax
from jax.experimental import pallas as pl
from jax.experimental.pallas import tpu as pltpu
from jax.sharding import PartitionSpec as P

F32 = jnp.float32
BF16 = jnp.bfloat16
AXES = ("tm", "space")
WID = 256
ROWS = 8
CH = 64
HID = 96
TWO = 2 * CH
FOUR = 4 * CH


def core_swap(x, tm):
    return lax.ppermute(x, "tm", [(i, i ^ 1) for i in range(tm)])


def side_swap(x, tm):
    return lax.ppermute(x, "tm", [(i, (((i + 1) ^ 1) - 1) % tm) for i in range(tm)])


def most_swap(x, tm):
    pairs = [(i, ((i + 1) ^ 1) - 1) for i in range(tm)]
    return lax.ppermute(x, "tm", [(i, j) for i, j in pairs if 0 <= j < tm and i + j != tm - 1])


def middle_swap(x, tm):
    low = tm // 2 - 1
    return lax.ppermute(x, "tm", [(low, low + 1), (low + 1, low)])


def row_swap(x, tm, space):
    pairs = []
    for t in range(tm):
        step = -1 if t % 2 == 0 else 1
        for s in range(space):
            inside = 0 <= s + step < space
            pairs.append((t * space + s, (t ^ 1) * space + s + step if inside else (t ^ 2) * space + s))
    return lax.ppermute(x, AXES, pairs)


def core_of():
    return lax.axis_index("tm") % 2


def silu(v):
    u = 0.5 * v
    return u + u * jnp.tanh(u)


def dot(a, b):
    return jnp.dot(a, b, preferred_element_type=F32)


def rows_first(block):
    return jnp.swapaxes(block.reshape(TWO, ROWS, WID), 0, 1)


def side_shifts(v):
    lane = lax.broadcasted_iota(jnp.int32, v.shape, v.ndim - 1)
    zero = jnp.zeros((), v.dtype)
    right = jnp.where(lane == 0, zero, pltpu.roll(v, 1, v.ndim - 1))
    left = jnp.where(lane == WID - 1, zero, pltpu.roll(v, WID - 1, v.ndim - 1))
    return right, left


def put_sides(dst, start, block):
    right, left = side_shifts(block)
    dst[0, pl.ds(start, block.shape[0])] = right
    dst[1, pl.ds(start, block.shape[0])] = left


def stacked(sides, *centre):
    return jnp.concatenate([sides[0], *centre, sides[1]], axis=0)


def put_hidden(dst, hid):
    hid = hid.astype(BF16)
    dst[0], dst[2] = side_shifts(hid)
    dst[1] = hid


def hidden_window(row_of, t, rows):
    return jnp.concatenate([row_of(i)[b, t * HID : (t + 1) * HID] for i in rows for b in range(3)], axis=0)


def add_estimates(acc, est_k, r, val):
    val = est_k * val
    for half in range(2):
        flat = acc.at[half].reshape(CH * ROWS, 128)
        for n in range(2):
            rows = pl.ds(r + n, CH, stride=ROWS)
            flat[rows, :] = flat[rows, :] + val[n * CH : (n + 1) * CH, half * 128 : (half + 1) * 128]


def prepare_kernel(
    states_ref,
    first_ref,
    second_ref,
    proj_ref,
    own_ref,
    w_near_ref,
    w_far_ref,
    w_two_ref,
    w_proj_ref,
    block_v,
    first_v,
    second_v,
    proj_v,
    sems,
):
    parts = block_v.shape[0]
    size = TWO // parts
    copies = []
    for n in range(parts):
        t, c = divmod(n * size, CH)
        copies.append(pltpu.make_async_copy(states_ref.at[t, pl.ds(c, size)], block_v.at[n], sems.at[n]))
    copies += [
        pltpu.make_async_copy(first_ref, first_v, sems.at[parts]),
        pltpu.make_async_copy(second_ref, second_v, sems.at[parts + 1]),
        pltpu.make_async_copy(proj_ref, proj_v, sems.at[parts + 2]),
    ]
    for copy in copies:
        copy.start()
    core = core_of()
    for n in range(parts):
        copies[n].wait()
        own_ref[:, n * size : (n + 1) * size] = jnp.swapaxes(block_v[n], 0, 1)
    for copy in copies[parts:]:
        copy.wait()
    blank = jnp.zeros((HID, CH), BF16)
    for n in range(9):
        block = first_v[n // 3, n % 3]
        for t, six in enumerate(([block, blank], [blank, block])):
            six = jnp.concatenate(six, axis=1)
            first, last = six[:, :TWO], six[:, FOUR:]
            rows = slice(t * HID, (t + 1) * HID)
            w_near_ref[rows, n * FOUR : n * FOUR + TWO] = six[:, TWO:FOUR]
            w_near_ref[rows, n * FOUR + TWO : (n + 1) * FOUR] = jnp.where(core == 0, last, first)
            w_far_ref[rows, n * TWO : (n + 1) * TWO] = jnp.where(core == 0, first, last)
    blank = jnp.zeros((HID, 3 * HID), BF16)
    w_two_ref[:HID, 9 * HID :] = blank
    w_two_ref[HID:, : 3 * HID] = blank
    for n in range(9):
        block = second_v[n // 3, n % 3]
        w_two_ref[:HID, n * HID : (n + 1) * HID] = block
        w_two_ref[HID:, (n + 3) * HID : (n + 4) * HID] = block
    blank = jnp.zeros((CH, HID), BF16)
    w_proj_ref[:CH] = jnp.concatenate([proj_v[...], blank], axis=1)
    w_proj_ref[CH:] = jnp.concatenate([blank, proj_v[...]], axis=1)


def edge_kernel(own_ref, partner_ref, edge_ref):
    core = core_of()
    other = partner_ref[...].reshape(TWO, ROWS, WID)
    other = jnp.swapaxes(jnp.where(core == 0, other[:, :2], other[:, ROWS - 2 :]), 0, 1)
    last = jnp.where(core == 0, 0, lax.axis_size("space") - 1)
    inside = lax.axis_index("space") != last
    zero = jnp.zeros((), BF16)
    mine = jnp.where(inside, own_ref[pl.ds(core * (ROWS - 2), 2)], zero)
    other = jnp.where(inside, other, zero)
    edge_ref[:, pl.ds(pl.multiple_of(core * TWO, TWO), TWO)] = mine
    edge_ref[:, pl.ds(pl.multiple_of((1 - core) * TWO, TWO), TWO)] = other


def at_end():
    at = lax.axis_index("tm")
    return (at == 0) | (at == lax.axis_size("tm") - 1)


def corner_kernel(rows_a_ref, rows_b_ref, send_ref):
    core = core_of()
    mine = pl.ds(pl.multiple_of(core * TWO, TWO), TWO)
    zero = jnp.zeros((), BF16)
    send_ref[pl.ds(core * 2, 2)] = jnp.where(at_end(), zero, rows_a_ref[:, mine])
    send_ref[pl.ds((1 - core) * 2, 2)] = jnp.where(at_end(), zero, rows_b_ref[:, mine])


def near_rows(sides_ref, own_ref, partner_rows_ref, *rows):
    return jnp.concatenate([stacked(sides_ref.at[l], own_ref[l], partner_rows_ref[l]) for l in rows], axis=0)


def near_kernel(own_ref, partner_ref, w_near_ref, partner_rows_ref, sides_ref, part_ref, edge_part_ref):
    partner_rows_ref[...] = rows_first(partner_ref[...])
    for l in range(ROWS):
        put_sides(sides_ref.at[l], 0, own_ref[l])
        put_sides(sides_ref.at[l], TWO, partner_rows_ref[l])
        if 2 <= l < part_ref.shape[0] + 2:
            part_ref[l - 2] = dot(w_near_ref[...], near_rows(sides_ref, own_ref, partner_rows_ref, l - 2, l - 1, l))
        if l == 1:
            edge_part_ref[0] = dot(w_near_ref[:, 3 * FOUR :], near_rows(sides_ref, own_ref, partner_rows_ref, 0, 1))
    edge_part_ref[1] = dot(w_near_ref[:, : 6 * FOUR], near_rows(sides_ref, own_ref, partner_rows_ref, 6, 7))


def rest_kernel(own_ref, partner_rows_ref, sides_ref, w_near_ref, part_ref):
    count = part_ref.shape[0]
    for n in range(count):
        r = ROWS - 1 - count + n
        window = near_rows(sides_ref, own_ref, partner_rows_ref, r - 1, r, r + 1)
        part_ref[n] = dot(w_near_ref[...], window)


def base_kernel(
    now_ref, next_ref, mask_ref, states_ref, observed_ref, noise_ref, base_ref, coef_ref
):
    level = jnp.full((ROWS, WID), now_ref[0], F32)
    later = jnp.full((ROWS, WID), next_ref[0], F32)
    drop = level * level - later * later
    coef_ref[0] = 1.0 / jnp.sqrt(1.0 + level * level)
    coef_ref[1] = -drop / level
    obs_k = drop / (0.1 + level * level)
    noise_k = jnp.sqrt(drop)
    for t in range(2):
        weight = mask_ref[t].astype(F32) * obs_k
        current = states_ref[t].astype(F32)
        seen = observed_ref[t].astype(F32)
        val = current + weight[None] * (seen - current) + noise_k[None] * noise_ref[t]
        base_ref[t, 0] = val[:, :, :128]
        base_ref[t, 1] = val[:, :, 128:]


def rim_kernel(
    rows_a_ref, rows_b_ref, own_ref, partner_rows_ref, near_ref, w_near_ref, edge_part_ref, part_ref, halo, sides
):
    core = core_of()
    own_at = pl.multiple_of(core * TWO, TWO)
    partner_at = pl.multiple_of((1 - core) * TWO, TWO)
    for l in range(2):
        for n, at in ((0, own_at), (1, partner_at)):
            a, b = rows_a_ref[l, pl.ds(at, TWO)], rows_b_ref[l, pl.ds(at, TWO)]
            halo[l, n * TWO : (n + 1) * TWO] = jnp.where(core == 0, a, b)
            halo[l + 2, n * TWO : (n + 1) * TWO] = jnp.where(core == 0, b, a)

    def tile(l):
        return stacked(near_ref.at[l], own_ref[l], partner_rows_ref[l])

    def outside(l):
        put_sides(sides.at[l], 0, halo[l])
        return stacked(sides.at[l], halo[l])

    def near(*rows):
        return dot(w_near_ref[...], jnp.concatenate(rows, axis=0))

    above, below = [outside(0), outside(1)], [outside(2), outside(3)]
    part_ref[0] = near(above[0], above[1], tile(0))
    part_ref[1] = edge_part_ref[0] + dot(w_near_ref[:, : 3 * FOUR], above[1])
    part_ref[2] = edge_part_ref[1] + dot(w_near_ref[:, 6 * FOUR :], below[0])
    part_ref[3] = near(tile(7), below[0], below[1])


def far_kernel(
    most_ref, middle_ref, part_ref, part_late_ref, rim_part_ref, w_far_ref, coef_ref, hid_ref, rim_out_ref, rows_v, sides
):
    scale = coef_ref[0][:1]
    at, size = lax.axis_index("tm"), lax.axis_size("tm")
    in_middle = (at == size // 2 - 1) | (at == size // 2)
    block = jnp.where(in_middle, middle_ref[...], most_ref[...])
    rows_v[...] = rows_first(jnp.where(at_end(), jnp.zeros((), BF16), block))

    def far(a, l, n):
        columns = slice(3 * a * TWO, 3 * (a + n) * TWO)
        rows = [stacked(sides.at[i], rows_v[i]) for i in range(l, l + n)]
        return dot(w_far_ref[:, columns], jnp.concatenate(rows, axis=0))

    for l in range(3):
        put_sides(sides.at[l], 0, rows_v[l])
    for r in range(1, ROWS - 1):
        if r + 2 < ROWS:
            put_sides(sides.at[r + 2], 0, rows_v[r + 2])
        early = part_ref.shape[0]
        part = part_ref[r - 1] if r <= early else part_late_ref[r - 1 - early]
        pre = part + far(0, r - 1, 3)
        put_hidden(hid_ref.at[r - 1], silu(pre * scale))
    rim_out_ref[0] = rim_part_ref[0] + far(2, 0, 1)
    rim_out_ref[1] = rim_part_ref[1] + far(1, 0, 2)
    rim_out_ref[2] = rim_part_ref[2] + far(0, ROWS - 2, 2)
    rim_out_ref[3] = rim_part_ref[3] + far(0, ROWS - 1, 1)


def middle_kernel(hid_ref, w_two_ref, proj_ref, coef_ref, base_ref, known_ref, acc_ref, h2s):
    est_k = coef_ref[1][:1]

    def row(r):
        return hid_ref.at[r - 1]

    spots = [(t, r) for t in range(2) for r in (2, 4)]
    for n, (t, r) in enumerate(spots):
        window = hidden_window(row, t, range(r - 1, r + 3))
        h2s[n] = silu(dot(w_two_ref[...], window)).astype(BF16)
    for t in range(2):
        known_ref[t, 0] = dot(w_two_ref[:, 6 * HID :], hidden_window(row, t, (1, 2)))
        known_ref[t, 1] = dot(w_two_ref[:, : 6 * HID], hidden_window(row, t, (ROWS - 3, ROWS - 2)))
    for n, (t, r) in enumerate(spots):
        add_estimates(acc_ref.at[t], est_k, r, dot(proj_ref[...], h2s[n]))


def outer_kernel(
    corner_ref,
    part_ref,
    w_far_ref,
    w_two_ref,
    proj_ref,
    coef_ref,
    known_ref,
    base_ref,
    out_ref,
    acc_ref,
    sides,
    hrim,
    h2s,
    sems,
):
    for l in range(4):
        put_sides(sides.at[l], 0, corner_ref[l])
    scale = coef_ref[0][:1]
    up = lax.axis_index("space") > 0
    down = lax.axis_index("space") < lax.axis_size("space") - 1

    def far(a, l, n):
        columns = slice(3 * a * TWO, 3 * (a + n) * TWO)
        rows = [stacked(sides.at[i], corner_ref[i]) for i in range(l, l + n)]
        return dot(w_far_ref[:, columns], jnp.concatenate(rows, axis=0))

    pre = [
        part_ref[0] + far(0, 0, 2),
        part_ref[1] + far(0, 1, 1),
        part_ref[2] + far(2, 2, 1),
        part_ref[3] + far(1, 2, 2),
    ]
    hid = [silu(p * scale) for p in pre]
    hid[0] = jnp.where(up, hid[0], 0.0)
    hid[3] = jnp.where(down, hid[3], 0.0)
    for l in range(4):
        put_hidden(hrim.at[l], hid[l])

    est_k = coef_ref[1][:1]
    spots = [(t, n) for n in range(2) for t in range(2)]
    weights = (w_two_ref[:, : 6 * HID], w_two_ref[:, 6 * HID :])
    for t, n in spots:
        window = hidden_window(lambda i: hrim.at[i], t, (2 * n, 2 * n + 1))
        h2s[t, n] = silu(known_ref[t, n] + dot(weights[n], window)).astype(BF16)
    vals = {(t, n): dot(proj_ref[...], h2s[t, n]) for t, n in spots}
    copies = []
    for t in range(2):
        for n in range(2):
            add_estimates(acc_ref.at[t], est_k, n * (ROWS - 2), vals[t, n])
        for half in range(2):
            target = out_ref.at[t, :, :, pl.ds(half * 128, 128)]
            copies.append(pltpu.make_async_copy(acc_ref.at[t, half], target, sems.at[2 * t + half]))
            copies[-1].start()
    for copy in copies:
        copy.wait()


VMEM = pl.BlockSpec(memory_space=pltpu.VMEM)
SMEM = pl.BlockSpec(memory_space=pltpu.SMEM)
ANY = pl.BlockSpec(memory_space=pl.ANY)
HBM = pl.BlockSpec(memory_space=pltpu.HBM)


def in_hbm(x):
    return pltpu.with_memory_space_constraint(x, pltpu.HBM)


def call(kernel, outs, ins, scratch=(), mib=4, flops=0, scalars=0, hbm=0, out_specs=None, alias=()):
    shapes = [jax.ShapeDtypeStruct(s, d) for s, d in outs]
    ins = list(ins[: len(ins) - hbm]) + [in_hbm(x) for x in ins[len(ins) - hbm :]]
    return pl.pallas_call(
        kernel,
        out_shape=shapes,
        in_specs=[SMEM] * scalars + [VMEM] * (len(ins) - scalars - hbm) + [HBM] * hbm,
        out_specs=out_specs or [VMEM] * len(shapes),
        scratch_shapes=scratch,
        input_output_aliases=dict(alias),
        compiler_params=pltpu.CompilerParams(vmem_limit_bytes=mib * 2**20),
        cost_estimate=pl.CostEstimate(flops=flops, bytes_accessed=2**20, transcendentals=0),
        name=kernel.__name__,
    )(*ins)


def body(
    states,
    observed,
    station_mask,
    noise,
    sigma_now,
    sigma_next,
    first_kernel,
    second_kernel,
    out_weight,
):
    tm, space = lax.axis_size("tm"), lax.axis_size("space")
    rows_shape = ((ROWS, TWO, WID), BF16)
    acc_shape = ((2, 2, CH, ROWS, 128), F32)
    partner = core_swap(states, tm)
    own, w_near, w_far, w_two, w_proj = call(
        prepare_kernel,
        [
            rows_shape,
            ((2 * HID, 9 * FOUR), BF16),
            ((2 * HID, 9 * TWO), BF16),
            ((2 * HID, 12 * HID), BF16),
            ((2 * CH, 2 * HID), BF16),
        ],
        [states, first_kernel, second_kernel, out_weight],
        [
            pltpu.VMEM((4, TWO // 4, ROWS, WID), BF16),
            pltpu.VMEM(first_kernel.shape, BF16),
            pltpu.VMEM(second_kernel.shape, BF16),
            pltpu.VMEM(out_weight.shape, BF16),
            pltpu.SemaphoreType.DMA((7,)),
        ],
        mib=8,
        hbm=4,
    )
    (edge,) = call(edge_kernel, [((2, FOUR, WID), BF16)], [own, partner])
    edge, states_x = lax.optimization_barrier((edge, states))
    rows_a = row_swap(edge, tm, space)
    most = most_swap(states_x, tm)
    early = 5
    partner_rows, near_sides, part, edge_part = call(
        near_kernel,
        [rows_shape, ((ROWS, 2, FOUR, WID), BF16), ((early, 2 * HID, WID), F32), ((2, 2 * HID, WID), F32)],
        [own, partner, w_near],
        mib=8,
        flops=2 * 10**9,
    )
    states_late, part = lax.optimization_barrier((states, part))
    middle = middle_swap(states_late, tm)
    (part_late,) = call(
        rest_kernel,
        [((ROWS - 2 - early, 2 * HID, WID), F32)],
        [own, partner_rows, near_sides, w_near],
        mib=8,
    )
    rows_a, part, part_late = lax.optimization_barrier((rows_a, part, part_late))
    rows_b = core_swap(rows_a, tm)
    (send,) = call(corner_kernel, [((4, TWO, WID), BF16)], [rows_a, rows_b])
    send, noise_late = lax.optimization_barrier((send, noise))
    base, coef = call(
        base_kernel,
        [acc_shape, ((2, ROWS, WID), F32)],
        [sigma_now, sigma_next, station_mask, states, observed, noise_late],
        flops=10**8,
        scalars=2,
    )
    corner = side_swap(send, tm)
    (rim_part,) = call(
        rim_kernel,
        [((4, 2 * HID, WID), F32)],
        [rows_a, rows_b, own, partner_rows, near_sides, w_near, edge_part],
        [pltpu.VMEM((4, FOUR, WID), BF16), pltpu.VMEM((4, 2, FOUR, WID), BF16)],
        mib=12,
        flops=10**9,
    )
    hid, rim_part = call(
        far_kernel,
        [((6, 3, 2 * HID, WID), BF16), ((4, 2 * HID, WID), F32)],
        [most, middle, part, part_late, rim_part, w_far, coef],
        [pltpu.VMEM((ROWS, TWO, WID), BF16), pltpu.VMEM((ROWS, 2, TWO, WID), BF16)],
        mib=8,
        flops=10**9,
    )
    known, acc = call(
        middle_kernel,
        [((2, 2, 2 * HID, WID), F32), acc_shape],
        [hid, w_two, w_proj, coef, base],
        [pltpu.VMEM((4, 2 * HID, WID), BF16)],
        mib=8,
        flops=10**9,
        alias=[(4, 1)],
    )
    out, _ = call(
        outer_kernel,
        [(noise.shape, F32), acc_shape],
        [corner, rim_part, w_far, w_two, w_proj, coef, known, acc],
        [
            pltpu.VMEM((4, 2, TWO, WID), BF16),
            pltpu.VMEM((4, 3, 2 * HID, WID), BF16),
            pltpu.VMEM((2, 2, 2 * HID, WID), BF16),
            pltpu.SemaphoreType.DMA((4,)),
        ],
        mib=12,
        flops=10**9,
        out_specs=[ANY, VMEM],
        alias=[(7, 1)],
    )
    return out


def solution(mesh):
    in_specs = (
        P("tm", None, "space", None),
        P("tm", None, "space", None),
        P("tm", "space", None),
        P("tm", None, "space", None),
        P(),
        P(),
        P(),
        P(),
        P(),
    )
    out_specs = P("tm", None, "space", None)
    return jax.shard_map(body, mesh=mesh, in_specs=in_specs, out_specs=out_specs, check_vma=False)
```

```python
import jax
import jax.numpy as jnp
from jax import lax
from jax.experimental import pallas as pl
from jax.experimental.pallas import tpu as pltpu
from jax.sharding import PartitionSpec as P

F32 = jnp.float32
BF16 = jnp.bfloat16
AXES = ("tm", "space")
WID = 256
ROWS = 8
CH = 64
HID = 96
TWO = 2 * CH
FOUR = 4 * CH


def core_swap(x, tm):
    return lax.ppermute(x, "tm", [(i, i ^ 1) for i in range(tm)])


def side_swap(x, tm):
    return lax.ppermute(x, "tm", [(i, (((i + 1) ^ 1) - 1) % tm) for i in range(tm)])


def most_swap(x, tm):
    pairs = [(i, ((i + 1) ^ 1) - 1) for i in range(tm)]
    return lax.ppermute(x, "tm", [(i, j) for i, j in pairs if 0 <= j < tm and i + j != tm - 1])


def middle_swap(x, tm):
    low = tm // 2 - 1
    return lax.ppermute(x, "tm", [(low, low + 1), (low + 1, low)])


def row_swap(x, tm, space):
    pairs = []
    for t in range(tm):
        step = -1 if t % 2 == 0 else 1
        for s in range(space):
            inside = 0 <= s + step < space
            pairs.append((t * space + s, (t ^ 1) * space + s + step if inside else (t ^ 2) * space + s))
    return lax.ppermute(x, AXES, pairs)


def core_of():
    return lax.axis_index("tm") % 2


def silu(v):
    u = 0.5 * v
    return u + u * jnp.tanh(u)


def dot(a, b):
    return jnp.dot(a, b, preferred_element_type=F32)


def rows_first(block):
    return jnp.swapaxes(block.reshape(TWO, ROWS, WID), 0, 1)


def side_shifts(v):
    lane = lax.broadcasted_iota(jnp.int32, v.shape, v.ndim - 1)
    zero = jnp.zeros((), v.dtype)
    right = jnp.where(lane == 0, zero, pltpu.roll(v, 1, v.ndim - 1))
    left = jnp.where(lane == WID - 1, zero, pltpu.roll(v, WID - 1, v.ndim - 1))
    return right, left


def put_sides(dst, start, block):
    right, left = side_shifts(block)
    dst[0, pl.ds(start, block.shape[0])] = right
    dst[1, pl.ds(start, block.shape[0])] = left


def stacked(sides, *centre):
    return jnp.concatenate([sides[0], *centre, sides[1]], axis=0)


def put_hidden(dst, hid):
    hid = hid.astype(BF16)
    dst[0], dst[2] = side_shifts(hid)
    dst[1] = hid


def hidden_window(row_of, t, rows):
    return jnp.concatenate([row_of(i)[b, t * HID : (t + 1) * HID] for i in rows for b in range(3)], axis=0)


def add_estimates(acc, est_k, r, val):
    val = est_k * val
    for half in range(2):
        flat = acc.at[half].reshape(CH * ROWS, 128)
        for n in range(2):
            rows = pl.ds(r + n, CH, stride=ROWS)
            flat[rows, :] = flat[rows, :] + val[n * CH : (n + 1) * CH, half * 128 : (half + 1) * 128]


def prepare_kernel(
    states_ref,
    first_ref,
    second_ref,
    proj_ref,
    own_ref,
    w_near_ref,
    w_far_ref,
    w_two_ref,
    w_proj_ref,
    block_v,
    first_v,
    second_v,
    proj_v,
    sems,
):
    parts = block_v.shape[0]
    size = TWO // parts
    copies = []
    for n in range(parts):
        t, c = divmod(n * size, CH)
        copies.append(pltpu.make_async_copy(states_ref.at[t, pl.ds(c, size)], block_v.at[n], sems.at[n]))
    copies += [
        pltpu.make_async_copy(first_ref, first_v, sems.at[parts]),
        pltpu.make_async_copy(second_ref, second_v, sems.at[parts + 1]),
        pltpu.make_async_copy(proj_ref, proj_v, sems.at[parts + 2]),
    ]
    for copy in copies:
        copy.start()
    core = core_of()
    for n in range(parts):
        copies[n].wait()
        own_ref[:, n * size : (n + 1) * size] = jnp.swapaxes(block_v[n], 0, 1)
    for copy in copies[parts:]:
        copy.wait()
    blank = jnp.zeros((HID, CH), BF16)
    for n in range(9):
        block = first_v[n // 3, n % 3]
        for t, six in enumerate(([block, blank], [blank, block])):
            six = jnp.concatenate(six, axis=1)
            first, last = six[:, :TWO], six[:, FOUR:]
            rows = slice(t * HID, (t + 1) * HID)
            w_near_ref[rows, n * FOUR : n * FOUR + TWO] = six[:, TWO:FOUR]
            w_near_ref[rows, n * FOUR + TWO : (n + 1) * FOUR] = jnp.where(core == 0, last, first)
            w_far_ref[rows, n * TWO : (n + 1) * TWO] = jnp.where(core == 0, first, last)
    blank = jnp.zeros((HID, 3 * HID), BF16)
    w_two_ref[:HID, 9 * HID :] = blank
    w_two_ref[HID:, : 3 * HID] = blank
    for n in range(9):
        block = second_v[n // 3, n % 3]
        w_two_ref[:HID, n * HID : (n + 1) * HID] = block
        w_two_ref[HID:, (n + 3) * HID : (n + 4) * HID] = block
    blank = jnp.zeros((CH, HID), BF16)
    w_proj_ref[:CH] = jnp.concatenate([proj_v[...], blank], axis=1)
    w_proj_ref[CH:] = jnp.concatenate([blank, proj_v[...]], axis=1)


def edge_kernel(own_ref, partner_ref, edge_ref):
    core = core_of()
    other = rows_first(partner_ref[...])
    last = jnp.where(core == 0, 0, lax.axis_size("space") - 1)
    inside = lax.axis_index("space") != last
    zero = jnp.zeros((), BF16)
    mine = jnp.where(inside, own_ref[pl.ds(core * (ROWS - 2), 2)], zero)
    other = jnp.where(inside, jnp.where(core == 0, other[:2], other[-2:]), zero)
    edge_ref[:, pl.ds(pl.multiple_of(core * TWO, TWO), TWO)] = mine
    edge_ref[:, pl.ds(pl.multiple_of((1 - core) * TWO, TWO), TWO)] = other


def at_end():
    at = lax.axis_index("tm")
    return (at == 0) | (at == lax.axis_size("tm") - 1)


def corner_kernel(rows_a_ref, rows_b_ref, send_ref):
    core = core_of()
    mine = pl.ds(pl.multiple_of(core * TWO, TWO), TWO)
    zero = jnp.zeros((), BF16)
    send_ref[pl.ds(core * 2, 2)] = jnp.where(at_end(), zero, rows_a_ref[:, mine])
    send_ref[pl.ds((1 - core) * 2, 2)] = jnp.where(at_end(), zero, rows_b_ref[:, mine])


def near_rows(sides_ref, own_ref, partner_rows_ref, *rows):
    return jnp.concatenate([stacked(sides_ref.at[l], own_ref[l], partner_rows_ref[l]) for l in rows], axis=0)


def near_kernel(own_ref, partner_ref, w_near_ref, partner_rows_ref, sides_ref, part_ref, edge_part_ref):
    partner_rows_ref[...] = rows_first(partner_ref[...])
    for l in range(ROWS):
        put_sides(sides_ref.at[l], 0, own_ref[l])
        put_sides(sides_ref.at[l], TWO, partner_rows_ref[l])
        if 2 <= l < part_ref.shape[0] + 2:
            part_ref[l - 2] = dot(w_near_ref[...], near_rows(sides_ref, own_ref, partner_rows_ref, l - 2, l - 1, l))
        if l == 1:
            edge_part_ref[0] = dot(w_near_ref[:, 3 * FOUR :], near_rows(sides_ref, own_ref, partner_rows_ref, 0, 1))
    edge_part_ref[1] = dot(w_near_ref[:, : 6 * FOUR], near_rows(sides_ref, own_ref, partner_rows_ref, 6, 7))


def rest_kernel(own_ref, partner_rows_ref, sides_ref, w_near_ref, part_ref):
    count = part_ref.shape[0]
    for n in range(count):
        r = ROWS - 1 - count + n
        window = near_rows(sides_ref, own_ref, partner_rows_ref, r - 1, r, r + 1)
        part_ref[n] = dot(w_near_ref[...], window)


def base_kernel(
    now_ref, next_ref, mask_ref, states_ref, observed_ref, noise_ref, base_ref, coef_ref
):
    level = jnp.full((ROWS, WID), now_ref[0], F32)
    later = jnp.full((ROWS, WID), next_ref[0], F32)
    drop = level * level - later * later
    coef_ref[0] = 1.0 / jnp.sqrt(1.0 + level * level)
    coef_ref[1] = -drop / level
    obs_k = drop / (0.1 + level * level)
    noise_k = jnp.sqrt(drop)
    for t in range(2):
        weight = mask_ref[t].astype(F32) * obs_k
        current = states_ref[t].astype(F32)
        seen = observed_ref[t].astype(F32)
        val = current + weight[None] * (seen - current) + noise_k[None] * noise_ref[t]
        base_ref[t, 0] = val[:, :, :128]
        base_ref[t, 1] = val[:, :, 128:]


def rim_kernel(
    rows_a_ref, rows_b_ref, own_ref, partner_rows_ref, near_ref, w_near_ref, edge_part_ref, part_ref, halo, sides
):
    core = core_of()
    own_at = pl.multiple_of(core * TWO, TWO)
    partner_at = pl.multiple_of((1 - core) * TWO, TWO)
    for l in range(2):
        for n, at in ((0, own_at), (1, partner_at)):
            a, b = rows_a_ref[l, pl.ds(at, TWO)], rows_b_ref[l, pl.ds(at, TWO)]
            halo[l, n * TWO : (n + 1) * TWO] = jnp.where(core == 0, a, b)
            halo[l + 2, n * TWO : (n + 1) * TWO] = jnp.where(core == 0, b, a)

    def tile(l):
        return stacked(near_ref.at[l], own_ref[l], partner_rows_ref[l])

    def outside(l):
        put_sides(sides.at[l], 0, halo[l])
        return stacked(sides.at[l], halo[l])

    def near(*rows):
        return dot(w_near_ref[...], jnp.concatenate(rows, axis=0))

    above, below = [outside(0), outside(1)], [outside(2), outside(3)]
    part_ref[0] = near(above[0], above[1], tile(0))
    part_ref[1] = edge_part_ref[0] + dot(w_near_ref[:, : 3 * FOUR], above[1])
    part_ref[2] = edge_part_ref[1] + dot(w_near_ref[:, 6 * FOUR :], below[0])
    part_ref[3] = near(tile(7), below[0], below[1])


def far_kernel(
    most_ref, middle_ref, part_ref, part_late_ref, rim_part_ref, w_far_ref, coef_ref, hid_ref, rim_out_ref, rows_v, sides
):
    scale = coef_ref[0][:1]
    at, size = lax.axis_index("tm"), lax.axis_size("tm")
    in_middle = (at == size // 2 - 1) | (at == size // 2)
    block = jnp.where(in_middle, middle_ref[...], most_ref[...])
    rows_v[...] = rows_first(jnp.where(at_end(), jnp.zeros((), BF16), block))

    def far(a, l, n):
        columns = slice(3 * a * TWO, 3 * (a + n) * TWO)
        rows = [stacked(sides.at[i], rows_v[i]) for i in range(l, l + n)]
        return dot(w_far_ref[:, columns], jnp.concatenate(rows, axis=0))

    for l in range(3):
        put_sides(sides.at[l], 0, rows_v[l])
    for r in range(1, ROWS - 1):
        if r + 2 < ROWS:
            put_sides(sides.at[r + 2], 0, rows_v[r + 2])
        early = part_ref.shape[0]
        part = part_ref[r - 1] if r <= early else part_late_ref[r - 1 - early]
        pre = part + far(0, r - 1, 3)
        put_hidden(hid_ref.at[r - 1], silu(pre * scale))
    rim_out_ref[0] = rim_part_ref[0] + far(2, 0, 1)
    rim_out_ref[1] = rim_part_ref[1] + far(1, 0, 2)
    rim_out_ref[2] = rim_part_ref[2] + far(0, ROWS - 2, 2)
    rim_out_ref[3] = rim_part_ref[3] + far(0, ROWS - 1, 1)


def middle_kernel(hid_ref, w_two_ref, proj_ref, coef_ref, base_ref, known_ref, acc_ref, h2s):
    est_k = coef_ref[1][:1]

    def row(r):
        return hid_ref.at[r - 1]

    spots = [(t, r) for t in range(2) for r in (2, 4)]
    for n, (t, r) in enumerate(spots):
        window = hidden_window(row, t, range(r - 1, r + 3))
        h2s[n] = silu(dot(w_two_ref[...], window)).astype(BF16)
    for t in range(2):
        known_ref[t, 0] = dot(w_two_ref[:, 6 * HID :], hidden_window(row, t, (1, 2)))
        known_ref[t, 1] = dot(w_two_ref[:, : 6 * HID], hidden_window(row, t, (ROWS - 3, ROWS - 2)))
    for n, (t, r) in enumerate(spots):
        add_estimates(acc_ref.at[t], est_k, r, dot(proj_ref[...], h2s[n]))


def outer_kernel(
    corner_ref,
    part_ref,
    w_far_ref,
    w_two_ref,
    proj_ref,
    coef_ref,
    known_ref,
    base_ref,
    out_ref,
    acc_ref,
    sides,
    hrim,
    h2s,
    sems,
):
    for l in range(4):
        put_sides(sides.at[l], 0, corner_ref[l])
    scale = coef_ref[0][:1]
    up = lax.axis_index("space") > 0
    down = lax.axis_index("space") < lax.axis_size("space") - 1

    def far(a, l, n):
        columns = slice(3 * a * TWO, 3 * (a + n) * TWO)
        rows = [stacked(sides.at[i], corner_ref[i]) for i in range(l, l + n)]
        return dot(w_far_ref[:, columns], jnp.concatenate(rows, axis=0))

    pre = [
        part_ref[0] + far(0, 0, 2),
        part_ref[1] + far(0, 1, 1),
        part_ref[2] + far(2, 2, 1),
        part_ref[3] + far(1, 2, 2),
    ]
    hid = [silu(p * scale) for p in pre]
    hid[0] = jnp.where(up, hid[0], 0.0)
    hid[3] = jnp.where(down, hid[3], 0.0)
    for l in range(4):
        put_hidden(hrim.at[l], hid[l])

    est_k = coef_ref[1][:1]
    spots = [(t, n) for n in range(2) for t in range(2)]
    weights = (w_two_ref[:, : 6 * HID], w_two_ref[:, 6 * HID :])
    for t, n in spots:
        window = hidden_window(lambda i: hrim.at[i], t, (2 * n, 2 * n + 1))
        h2s[t, n] = silu(known_ref[t, n] + dot(weights[n], window)).astype(BF16)
    for t, n in spots:
        add_estimates(acc_ref.at[t], est_k, n * (ROWS - 2), dot(proj_ref[...], h2s[t, n]))
    copies = []
    for t, half in spots:
        target = out_ref.at[t, :, :, pl.ds(half * 128, 128)]
        copies.append(pltpu.make_async_copy(acc_ref.at[t, half], target, sems.at[2 * t + half]))
        copies[-1].start()
    for copy in copies:
        copy.wait()


VMEM = pl.BlockSpec(memory_space=pltpu.VMEM)
SMEM = pl.BlockSpec(memory_space=pltpu.SMEM)
ANY = pl.BlockSpec(memory_space=pl.ANY)
HBM = pl.BlockSpec(memory_space=pltpu.HBM)


def in_hbm(x):
    return pltpu.with_memory_space_constraint(x, pltpu.HBM)


def call(kernel, outs, ins, scratch=(), mib=4, flops=0, scalars=0, hbm=0, out_specs=None, alias=()):
    shapes = [jax.ShapeDtypeStruct(s, d) for s, d in outs]
    ins = list(ins[: len(ins) - hbm]) + [in_hbm(x) for x in ins[len(ins) - hbm :]]
    return pl.pallas_call(
        kernel,
        out_shape=shapes,
        in_specs=[SMEM] * scalars + [VMEM] * (len(ins) - scalars - hbm) + [HBM] * hbm,
        out_specs=out_specs or [VMEM] * len(shapes),
        scratch_shapes=scratch,
        input_output_aliases=dict(alias),
        compiler_params=pltpu.CompilerParams(vmem_limit_bytes=mib * 2**20),
        cost_estimate=pl.CostEstimate(flops=flops, bytes_accessed=2**20, transcendentals=0),
        name=kernel.__name__,
    )(*ins)


def body(
    states,
    observed,
    station_mask,
    noise,
    sigma_now,
    sigma_next,
    first_kernel,
    second_kernel,
    out_weight,
):
    tm, space = lax.axis_size("tm"), lax.axis_size("space")
    rows_shape = ((ROWS, TWO, WID), BF16)
    acc_shape = ((2, 2, CH, ROWS, 128), F32)
    partner = core_swap(states, tm)
    own, w_near, w_far, w_two, w_proj = call(
        prepare_kernel,
        [
            rows_shape,
            ((2 * HID, 9 * FOUR), BF16),
            ((2 * HID, 9 * TWO), BF16),
            ((2 * HID, 12 * HID), BF16),
            ((2 * CH, 2 * HID), BF16),
        ],
        [states, first_kernel, second_kernel, out_weight],
        [
            pltpu.VMEM((4, TWO // 4, ROWS, WID), BF16),
            pltpu.VMEM(first_kernel.shape, BF16),
            pltpu.VMEM(second_kernel.shape, BF16),
            pltpu.VMEM(out_weight.shape, BF16),
            pltpu.SemaphoreType.DMA((7,)),
        ],
        mib=8,
        hbm=4,
    )
    (edge,) = call(edge_kernel, [((2, FOUR, WID), BF16)], [own, partner])
    edge, states_x = lax.optimization_barrier((edge, states))
    rows_a = row_swap(edge, tm, space)
    most = most_swap(states_x, tm)
    early = 5
    partner_rows, near_sides, part, edge_part = call(
        near_kernel,
        [rows_shape, ((ROWS, 2, FOUR, WID), BF16), ((early, 2 * HID, WID), F32), ((2, 2 * HID, WID), F32)],
        [own, partner, w_near],
        mib=8,
        flops=2 * 10**9,
    )
    states_late, part = lax.optimization_barrier((states, part))
    middle = middle_swap(states_late, tm)
    (part_late,) = call(
        rest_kernel,
        [((ROWS - 2 - early, 2 * HID, WID), F32)],
        [own, partner_rows, near_sides, w_near],
        mib=8,
    )
    rows_a, part, part_late = lax.optimization_barrier((rows_a, part, part_late))
    rows_b = core_swap(rows_a, tm)
    (send,) = call(corner_kernel, [((4, TWO, WID), BF16)], [rows_a, rows_b])
    send, noise_late = lax.optimization_barrier((send, noise))
    base, coef = call(
        base_kernel,
        [acc_shape, ((2, ROWS, WID), F32)],
        [sigma_now, sigma_next, station_mask, states, observed, noise_late],
        flops=10**8,
        scalars=2,
    )
    corner = side_swap(send, tm)
    (rim_part,) = call(
        rim_kernel,
        [((4, 2 * HID, WID), F32)],
        [rows_a, rows_b, own, partner_rows, near_sides, w_near, edge_part],
        [pltpu.VMEM((4, FOUR, WID), BF16), pltpu.VMEM((4, 2, FOUR, WID), BF16)],
        mib=12,
        flops=10**9,
    )
    hid, rim_part = call(
        far_kernel,
        [((6, 3, 2 * HID, WID), BF16), ((4, 2 * HID, WID), F32)],
        [most, middle, part, part_late, rim_part, w_far, coef],
        [pltpu.VMEM((ROWS, TWO, WID), BF16), pltpu.VMEM((ROWS, 2, TWO, WID), BF16)],
        mib=8,
        flops=10**9,
    )
    known, acc = call(
        middle_kernel,
        [((2, 2, 2 * HID, WID), F32), acc_shape],
        [hid, w_two, w_proj, coef, base],
        [pltpu.VMEM((4, 2 * HID, WID), BF16)],
        mib=8,
        flops=10**9,
        alias=[(4, 1)],
    )
    out, _ = call(
        outer_kernel,
        [(noise.shape, F32), acc_shape],
        [corner, rim_part, w_far, w_two, w_proj, coef, known, acc],
        [
            pltpu.VMEM((4, 2, TWO, WID), BF16),
            pltpu.VMEM((4, 3, 2 * HID, WID), BF16),
            pltpu.VMEM((2, 2, 2 * HID, WID), BF16),
            pltpu.SemaphoreType.DMA((4,)),
        ],
        mib=12,
        flops=10**9,
        out_specs=[ANY, VMEM],
        alias=[(7, 1)],
    )
    return out


def solution(mesh):
    in_specs = (
        P("tm", None, "space", None),
        P("tm", None, "space", None),
        P("tm", "space", None),
        P("tm", None, "space", None),
        P(),
        P(),
        P(),
        P(),
        P(),
    )
    out_specs = P("tm", None, "space", None)
    return jax.shard_map(body, mesh=mesh, in_specs=in_specs, out_specs=out_specs, check_vma=False)
```
